256 devices in a mesh: blk: 64 (over x, z, core), rep: 4 (over y).
Axes of the slice: x: 4, y: 4, z: 8, core: 2. Of those that a mesh axis runs over, the one named last changes fastest.
Arguments:
- source: bfloat16 [512, 512, 256], P('blk'), may hold values from -2 to 2
- targets: bfloat16 [256, 512, 256], P('blk', 'rep'), may hold values from -2 to 2
- log_a: float32 [512, 512], P('blk'), may hold values from -2 to 2
- log_b: float32 [256, 512], P('blk', 'rep'), may hold values from -2 to 2
- pair_source: int32 [64, 48], replicated, may hold values from 0 to 7, as said below
- pair_target: int32 [64, 48], replicated, may hold values from 0 to 255, as said below
- pair_count: int32 [64], replicated, may hold values from 24 to 48, as said below
Outputs:
- source_potential: float32 [512, 512], P('blk')
- target_potential: float32 [256, 512], P('blk', 'rep')
The draws below stay inside these ranges and needn't reach their ends.
Inputs may be any that keep to these rules, and one draw needn't show every extreme that they name: Owner o has pair_count[o] live pairs; one owner has exactly 48. `pair_source`: every one of an owner's 8 source blocks is named by one of its live pairs. Slots past the live count hold valid numbers and are unused. `pair_target`: target block t belongs to owner t // 4. An owner's live pairs name at most one block of each target owner, no live pair repeats within an owner, and every target block is named by some live pair. Slots past the live count hold valid numbers and are unused.
All inputs are finite; a program needn't handle non-finite values.
Results may differ from the reference program's by a relative error of at most 0.0003.
Values may be sent and summed in bfloat16 or wider, within the bound.
No kernel may reach another device: no remote copies, remote signals or barrier semaphores. Data moves between devices by JAX's collectives and lax.ppermute only.
A program may use at most 128 MiB of HBM per device.

```python
import jax
import jax.numpy as jnp
from jax import lax

E = 256
B = 512
SB = 8
TB = 4
ITERS = 2
SLOTS = 48
SBLOCKS = 512
TBLOCKS = 256
N_BLK = 64


def pair_tables(key):
    subkeys = jax.random.split(jax.random.fold_in(key, 101), 5)
    owner_ids = jnp.arange(N_BLK, dtype=jnp.int32)
    live_count = jax.random.randint(subkeys[0], (N_BLK,), 3 * SB, 5 * SB + 1).astype(jnp.int32)
    busiest = jax.random.randint(subkeys[1], (), 0, N_BLK)
    live_count = jnp.where(owner_ids == busiest, SLOTS, live_count).astype(jnp.int32)
    remaining = jax.vmap(lambda sub_key: jax.random.permutation(sub_key, N_BLK - TB))(jax.random.split(subkeys[2], N_BLK))
    offsets = jnp.concatenate([jnp.broadcast_to(jnp.arange(TB, dtype=jnp.int32), (N_BLK, TB)), (remaining + TB).astype(jnp.int32)], axis=1)
    slot_ids = jnp.arange(SLOTS, dtype=jnp.int32)
    position = slot_ids % N_BLK
    shifted = offsets[:, position]
    target_owner = (owner_ids[:, None] + shifted) % N_BLK
    chosen = jax.random.randint(subkeys[3], (N_BLK, N_BLK), 0, TB).astype(jnp.int32)
    local_block = jnp.where(position[None, :] < TB, position[None, :], chosen[:, position])
    target = (target_owner * TB + local_block).astype(jnp.int32)
    rotation = jax.random.randint(subkeys[4], (N_BLK,), 0, SB).astype(jnp.int32)
    source = ((slot_ids[None, :] + slot_ids[None, :] // N_BLK + rotation[:, None]) % SB).astype(jnp.int32)
    return (source, target, live_count)


def embedding_rows(key, count, spread):
    subkeys = jax.random.split(key, 3)
    normal_part = jax.random.normal(subkeys[0], (count, B, E), jnp.float32)
    base_rows = normal_part
    row_scale = jnp.exp(jax.random.uniform(subkeys[2], (count, B, 1), jnp.float32, -spread, 0.5 * spread))
    return 0.15 * base_rows * row_scale


def target_rows(key, spread):
    drawn = embedding_rows(jax.random.fold_in(key, 202), TBLOCKS, spread)
    return drawn


def draw_targets(key, part):
    return target_rows(key, 0.6).astype(jnp.bfloat16)


def draw_source(key, part):
    own_key = jax.random.fold_in(key, 303)
    drawn = embedding_rows(own_key, SBLOCKS, 0.6)
    return drawn.astype(jnp.bfloat16)


def draw_pair_source(key, part):
    return pair_tables(key)[0]


def draw_pair_target(key, part):
    return pair_tables(key)[1]


def draw_pair_count(key, part):
    return pair_tables(key)[2]


def shard_levels(rng, dims, cuts, smallest, largest):
    def one(axis_at, shards_of):
        draws = jax.random.uniform(jax.random.fold_in(jax.random.fold_in(rng, 6), axis_at), (shards_of,), jnp.float32, smallest / len(cuts), largest / len(cuts))
        return jnp.repeat(jnp.exp(draws), dims[axis_at] // shards_of).reshape((-1,) + (1,) * (len(dims) - axis_at - 1))

    loudness = one(*cuts[0])
    for cut in cuts[1:]:
        loudness = loudness * one(*cut)
    return loudness


def setup_inputs(seed: int = 0) -> dict:
    key_of = jax.random.split(jax.random.key(seed), 8)
    source = draw_source(jax.random.fold_in(key_of[7], 71), 0)
    targets = draw_targets(jax.random.fold_in(key_of[7], 71), 0)
    log_a = jnp.clip(jax.random.uniform(key_of[2], (SBLOCKS, B), jnp.float32, -2.0, 2.0) * shard_levels(key_of[2], (SBLOCKS, B), ((0, 64),), -0.4, 0.0), -2.0, 2.0)
    log_b = jnp.clip(jax.random.uniform(key_of[3], (TBLOCKS, B), jnp.float32, -2.0, 2.0) * shard_levels(key_of[3], (TBLOCKS, B), ((0, 64), (1, 4)), -0.4, 0.0), -2.0, 2.0)
    pair_source = draw_pair_source(jax.random.fold_in(key_of[7], 71), 0)
    pair_target = draw_pair_target(jax.random.fold_in(key_of[7], 71), 0)
    pair_count = draw_pair_count(jax.random.fold_in(key_of[7], 71), 0)
    return dict(source=source, targets=targets, log_a=log_a, log_b=log_b, pair_source=pair_source, pair_target=pair_target, pair_count=pair_count)


epsilon = 0.1
floor_value = -1e30


def tile_dot(source, targets, source_id, target_id):
    left = lax.dynamic_index_in_dim(source, source_id, 0, keepdims=False).astype(jnp.float32)
    right = lax.dynamic_index_in_dim(targets, target_id, 0, keepdims=False).astype(jnp.float32)
    return jnp.dot(left, right.T, precision=lax.Precision.HIGHEST)


def reference(source, targets, log_a, log_b, pair_source, pair_target, pair_count):
    slot_ids = jnp.arange(N_BLK * SLOTS, dtype=jnp.int32)
    owner_ids = (slot_ids // SLOTS).astype(jnp.int32)
    live_slots = (slot_ids % SLOTS) < pair_count[owner_ids]
    source_ids = (owner_ids * SB + pair_source.reshape(-1)).astype(jnp.int32)
    target_ids = pair_target.reshape(-1).astype(jnp.int32)

    def gathered(potentials, by_rows):
        length = SBLOCKS if by_rows else TBLOCKS
        initial = (jnp.full((length, B), floor_value, jnp.float32), jnp.zeros((length, B), jnp.float32))

        def advance(running, pair_item):
            source_id, target_id, live = pair_item

            def absorb_tile(state):
                highest, total = state
                dots = tile_dot(source, targets, source_id, target_id)
                if by_rows:
                    scores = (potentials[target_id][None, :] + dots) / epsilon
                    axis_of = 1
                    own_id = source_id
                else:
                    scores = (potentials[source_id][:, None] + dots) / epsilon
                    axis_of = 0
                    own_id = target_id
                tile_max = jnp.max(scores, axis=axis_of)
                tile_sum = jnp.sum(jnp.exp(scores - jnp.expand_dims(tile_max, axis_of)), axis=axis_of)
                before = highest[own_id]
                raised = jnp.maximum(before, tile_max)
                updated = total[own_id] * jnp.exp(before - raised) + tile_sum * jnp.exp(tile_max - raised)
                return highest.at[own_id].set(raised), total.at[own_id].set(updated)

            return lax.cond(live, absorb_tile, lambda state: state, running), None

        (highest, total), _ = lax.scan(advance, initial, (source_ids, target_ids, live_slots))
        return highest + jnp.log(total)

    target_potential = jnp.zeros((TBLOCKS, B), jnp.float32)
    source_potential = jnp.zeros((SBLOCKS, B), jnp.float32)
    for iteration in range(ITERS):
        source_potential = epsilon * log_a - epsilon * gathered(target_potential, True)
        target_potential = epsilon * log_b - epsilon * gathered(source_potential, False)
    return source_potential, target_potential
```

```python
import jax
import jax.numpy as jnp
from jax import lax
from jax.experimental import pallas as pl
from jax.experimental.pallas import tpu as pltpu
from jax.sharding import PartitionSpec as P

epsilon = 0.1
inv_epsilon = 10.0
floor_value = -1e30
sum_low, sum_high = 1e-13, 1e26
pot_low, pot_high = -80.0, 35.0
VMEM_LIMIT = 56 * 1024 * 1024

VM = pl.BlockSpec(memory_space=pltpu.VMEM)
SM = pl.BlockSpec(memory_space=pltpu.SMEM)
ANY = pl.BlockSpec(memory_space=pl.ANY)


def tile_dot(left, right):
    return lax.dot_general(left, right, (((1,), (1,)), ((), ())), preferred_element_type=jnp.float32)


def all_true(mask):
    return jnp.min(jnp.where(mask, 1.0, 0.0)) > 0.5


def lanes_to_row(tile, reduce):
    return reduce(tile.T, axis=0, keepdims=True)


def row_to_lanes(row):
    return jnp.broadcast_to(row, (128, row.shape[1])).T


def exact_rows(ps, pt, count, src, fet, g_ref, left, right, total, peak, lse_ref):
    total[...] = jnp.zeros(total.shape, jnp.float32)
    peak[...] = jnp.full(peak.shape, floor_value, jnp.float32)

    def step(p, _):
        s = ps[p]
        t = pt[p]
        pltpu.sync_copy(src.at[s], left)
        pltpu.sync_copy(fet.at[t], right)
        x = tile_dot(left[...], right[...])
        if g_ref is not None:
            x = x + g_ref[pl.ds(t // 4, 1), :]
        x = x * inv_epsilon
        before = peak[s]
        raised = jnp.maximum(before, x)
        total[s] = total[s] * jnp.exp(before - raised) + jnp.exp(x - raised)
        peak[s] = raised
        return 0

    lax.fori_loop(0, count, step, 0)
    for s in range(total.shape[0]):
        m = peak[s].T
        top = jnp.max(m, axis=0, keepdims=True)
        mass = jnp.sum(total[s].T * jnp.exp(m - top), axis=0, keepdims=True)
        lse_ref[pl.ds(s, 1), :] = top + jnp.log(mass)


def finish_rows(total, lse_ref):
    ok = jnp.ones((1, lse_ref.shape[1]), jnp.float32)
    for s in range(total.shape[0]):
        mass = lanes_to_row(total[s], jnp.sum)
        ok = jnp.minimum(ok, jnp.where((mass >= sum_low) & (mass <= sum_high), 1.0, 0.0))
        lse_ref[pl.ds(s, 1), :] = jnp.log(mass)
    return jnp.min(ok) > 0.5


def first_kernel(cnt, ps, pt, src, src_any, fet, k_out, lse_ref, tbuf, kbuf, total, peak, left, right, sin, sout):
    count = cnt[0]

    def fetch(p):
        return pltpu.make_async_copy(fet.at[pt[p]], tbuf.at[p], sin.at[p])

    def store(p):
        return pltpu.make_async_copy(kbuf.at[p], k_out.at[p], sout.at[p])

    lax.fori_loop(0, count, lambda p, c: (fetch(p).start(), c)[1], 0)
    total[...] = jnp.zeros(total.shape, jnp.float32)

    def step(p, _):
        fetch(p).wait()
        s = ps[p]
        k = jnp.exp(tile_dot(src[s], tbuf[p]) * inv_epsilon)
        kbuf[p] = k
        total[s] = total[s] + k
        store(p).start()
        return 0

    lax.fori_loop(0, count, step, 0)
    ok = finish_rows(total, lse_ref)
    lax.fori_loop(0, count, lambda p, c: (store(p).wait(), c)[1], 0)

    @pl.when(jnp.logical_not(ok))
    def _():
        exact_rows(ps, pt, count, src_any, fet, None, left, right, total, peak, lse_ref)


def row_kernel(cnt, ps, pt, g_ref, k_in, src_any, fet, lse_ref, vbuf, kbuf, total, peak, left, right, sin):
    count = cnt[0]

    def fetch(p):
        return pltpu.make_async_copy(k_in.at[p], kbuf.at[p], sin.at[p])

    lax.fori_loop(0, count, lambda p, c: (fetch(p).start(), c)[1], 0)
    total[...] = jnp.zeros(total.shape, jnp.float32)
    scaled = g_ref[...] * inv_epsilon
    vbuf[...] = jnp.exp(scaled)
    fits = all_true((scaled >= pot_low) & (scaled <= pot_high))

    def step(p, _):
        fetch(p).wait()
        s = ps[p]
        total[s] = total[s] + kbuf[p] * vbuf[pl.ds(pt[p] // 4, 1), :]
        return 0

    lax.fori_loop(0, count, step, 0)
    ok = finish_rows(total, lse_ref)

    @pl.when(jnp.logical_not(ok & fits))
    def _():
        exact_rows(ps, pt, count, src_any, fet, g_ref, left, right, total, peak, lse_ref)


def column_kernel(
    cnt, ps, pt, l0, l1, l2, l3, log_a, k_in, src_any, fet, f_ref, lse_ref, ubuf, kbuf, mass, left, right, sin
):
    count = cnt[0]

    def fetch(p):
        return pltpu.make_async_copy(k_in.at[p], kbuf.at[p], sin.at[p])

    lax.fori_loop(0, count, lambda p, c: (fetch(p).start(), c)[1], 0)
    a, b, c, d = l0[...], l1[...], l2[...], l3[...]
    top = jnp.maximum(jnp.maximum(a, c), jnp.maximum(b, d))
    summed = (jnp.exp(a - top) + jnp.exp(c - top)) + (jnp.exp(b - top) + jnp.exp(d - top))
    f = epsilon * log_a[...] - epsilon * (top + jnp.log(summed))
    f_ref[...] = f
    scaled = f * inv_epsilon
    fits = all_true((scaled >= pot_low) & (scaled <= pot_high))
    u = jnp.exp(scaled)
    for s in range(ubuf.shape[0]):
        ubuf[s] = row_to_lanes(u[s : s + 1, :])
    mass[...] = jnp.full(mass.shape, -1.0, jnp.float32)

    def step(p, _):
        fetch(p).wait()
        mass[pl.ds(pt[p] // 4, 1), :] = jnp.sum(kbuf[p] * ubuf[ps[p]], axis=0, keepdims=True)
        return 0

    lax.fori_loop(0, count, step, 0)
    m = mass[...]
    dead = m == -1.0
    ok = all_true(dead | ((m >= sum_low) & (m <= sum_high)))
    lse_ref[...] = jnp.where(dead, floor_value, jnp.log(m))

    @pl.when(jnp.logical_not(ok & fits))
    def _():
        for s in range(ubuf.shape[0]):
            ubuf[s] = row_to_lanes(f[s : s + 1, :])

        def exact(p, _):
            s = ps[p]
            t = pt[p]
            pltpu.sync_copy(src_any.at[s], left)
            pltpu.sync_copy(fet.at[t], right)
            x = (ubuf[s] + tile_dot(left[...], right[...])) * inv_epsilon
            high = jnp.max(x, axis=0, keepdims=True)
            lse_ref[pl.ds(t // 4, 1), :] = high + jnp.log(jnp.sum(jnp.exp(x - high), axis=0, keepdims=True))
            return 0

        lax.fori_loop(0, count, exact, 0)


def owner_kernel(parts, wanted, log_b, g_ref, back):
    x = parts[...]
    w = wanted[...]
    out = jnp.zeros(x.shape, jnp.float32)
    for j in range(g_ref.shape[0]):
        hit = jnp.broadcast_to(w, x.shape) == j
        top = jnp.max(jnp.where(hit, x, floor_value), axis=0, keepdims=True)
        mass = jnp.sum(jnp.where(hit, jnp.exp(x - top), 0.0), axis=0, keepdims=True)
        g = epsilon * log_b[pl.ds(j, 1), :] - epsilon * (top + jnp.log(mass))
        g_ref[pl.ds(j, 1), :] = g
        out = jnp.where(hit, g, out)
    back[...] = out


def per_device(source, targets, log_a, log_b, pair_source, pair_target, pair_count):
    self_index = lax.axis_index("blk")
    owners = lax.axis_size("blk")
    reps = lax.axis_size("rep")
    local_blocks, quarter, width = targets.shape
    blocks, rows, _ = source.shape
    slots = pair_source.shape[1]
    f32 = jnp.float32
    sds = jax.ShapeDtypeStruct
    params = pltpu.CompilerParams(vmem_limit_bytes=VMEM_LIMIT)

    live = lax.broadcasted_iota(jnp.int32, pair_target.shape, 1) < pair_count[:, None]
    asked = live & (pair_target // local_blocks == self_index)
    wanted = jnp.max(jnp.where(asked, pair_target % local_blocks, -1), axis=1, keepdims=True)
    ps = lax.dynamic_index_in_dim(pair_source, self_index, 0, keepdims=False)
    pt = lax.dynamic_index_in_dim(pair_target, self_index, 0, keepdims=False)
    cnt = lax.dynamic_slice_in_dim(pair_count, self_index, 1, 0)

    fetched = lax.all_gather(targets, "blk", axis=0, tiled=True)

    tiles = (slots, rows, quarter)
    exact_scratch = [pltpu.VMEM((rows, width), jnp.bfloat16), pltpu.VMEM((quarter, width), jnp.bfloat16)]
    acc = pltpu.VMEM((blocks, rows, quarter), f32)
    sems = pltpu.SemaphoreType.DMA((slots,))

    k_tiles, part = pl.pallas_call(
        first_kernel,
        out_shape=(sds(tiles, f32), sds((blocks, rows), f32)),
        in_specs=[SM, SM, SM, VM, ANY, ANY],
        out_specs=(ANY, VM),
        scratch_shapes=[
            pltpu.VMEM((slots, quarter, width), jnp.bfloat16),
            pltpu.VMEM(tiles, f32),
            acc,
            acc,
            *exact_scratch,
            sems,
            sems,
        ],
        compiler_params=params,
    )(cnt, ps, pt, source, source, fetched)

    def columns(part):
        parts = [part] + [
            lax.ppermute(part, "rep", [(i, (i + k) % reps) for i in range(reps)]) for k in range(1, reps)
        ]
        return pl.pallas_call(
            column_kernel,
            out_shape=(sds((blocks, rows), f32), sds((owners, quarter), f32)),
            in_specs=[SM, SM, SM, VM, VM, VM, VM, VM, ANY, ANY, ANY],
            out_specs=(VM, VM),
            scratch_shapes=[acc, pltpu.VMEM(tiles, f32), pltpu.VMEM((owners, quarter), f32), *exact_scratch, sems],
            compiler_params=params,
        )(cnt, ps, pt, *parts, log_a, k_tiles, source, fetched)

    def swap(x):
        return lax.all_to_all(x, "blk", split_axis=0, concat_axis=0, tiled=True)

    def owner(parts):
        return pl.pallas_call(
            owner_kernel,
            out_shape=(sds((local_blocks, quarter), f32), sds((owners, quarter), f32)),
            in_specs=[VM, VM, VM],
            out_specs=(VM, VM),
        )(parts, wanted, log_b)

    f, col = columns(part)
    g, back = owner(swap(col))
    part = pl.pallas_call(
        row_kernel,
        out_shape=sds((blocks, rows), f32),
        in_specs=[SM, SM, SM, VM, ANY, ANY, ANY],
        out_specs=VM,
        scratch_shapes=[
            pltpu.VMEM((owners, quarter), f32),
            pltpu.VMEM(tiles, f32),
            acc,
            acc,
            *exact_scratch,
            sems,
        ],
        compiler_params=params,
    )(cnt, ps, pt, swap(back), k_tiles, source, fetched)
    f, col = columns(part)
    g, _ = owner(swap(col))
    return f, g


def solution(mesh):
    in_specs = (
        P("blk", None, None),
        P("blk", "rep", None),
        P("blk", None),
        P("blk", "rep"),
        P(),
        P(),
        P(),
    )
    out_specs = (P("blk", None), P("blk", "rep"))
    return jax.shard_map(per_device, mesh=mesh, in_specs=in_specs, out_specs=out_specs, check_vma=False)
```

```python
import functools

import jax
import jax.numpy as jnp
import numpy as np
from jax import lax
from jax.experimental import pallas as pl
from jax.experimental.pallas import tpu as pltpu
from jax.sharding import Mesh, PartitionSpec as P

epsilon = 0.1
inv_epsilon = 10.0
floor_value = -1e30
sum_low, sum_high = 1e-13, 1e26
pot_low, pot_high = -80.0, 35.0
VMEM_LIMIT = 56 * 1024 * 1024

VM = pl.BlockSpec(memory_space=pltpu.VMEM)
SM = pl.BlockSpec(memory_space=pltpu.SMEM)
ANY = pl.BlockSpec(memory_space=pl.ANY)

XS, ZS = 4, 8
CHIPS = XS * ZS
DX = (0, 1, 3, 2)
DZ = (0, 1, 7, 2, 6, 3, 5, 4)
NEAR = 3
SLOTS = 2 * CHIPS
NEAR_SLOTS = 2 * NEAR * XS
ROWS_A = 48
CODE, LIST, TROW, HAS, COUNTS, TABLE = 0, 64, 128, 160, 176, 192


def tile_dot(left, right):
    return lax.dot_general(left, right, (((1,), (1,)), ((), ())), preferred_element_type=jnp.float32)


def all_true(mask):
    return jnp.min(jnp.where(mask, 1.0, 0.0)) > 0.5


def row_to_lanes(row):
    return jnp.broadcast_to(row, (128, row.shape[1])).T


def pair_of(tab, i):
    slot = tab[LIST + i]
    h = slot & 1
    return slot, h * 8 + (tab[CODE + slot] >> 2), h * CHIPS + tab[TROW + (slot >> 1)]


def load_source(own, sib, s, left):
    @pl.when(s < 8)
    def _():
        pltpu.sync_copy(own.at[s & 7], left)

    @pl.when(s >= 8)
    def _():
        pltpu.sync_copy(sib.at[s & 7], left)


def exact_rows(tab, own, sib, tt, g_ref, left, right, total, peak, lse_ref):
    total[...] = jnp.zeros(total.shape, jnp.float32)
    peak[...] = jnp.full(peak.shape, floor_value, jnp.float32)

    def step(i, _):
        slot, s, t = pair_of(tab, i)
        load_source(own, sib, s, left)
        pltpu.sync_copy(tt.at[slot], right)
        x = tile_dot(left[...], right[...])
        if g_ref is not None:
            x = x + g_ref[pl.ds(t, 1), :]
        x = x * inv_epsilon
        before = peak[s]
        raised = jnp.maximum(before, x)
        total[s] = total[s] * jnp.exp(before - raised) + jnp.exp(x - raised)
        peak[s] = raised
        return 0

    lax.fori_loop(0, tab[COUNTS + 1], step, 0)
    for s in range(total.shape[0]):
        m = peak[s].T
        top = jnp.max(m, axis=0, keepdims=True)
        mass = jnp.sum(total[s].T * jnp.exp(m - top), axis=0, keepdims=True)
        lse_ref[pl.ds(s, 1), :] = jnp.where(tab[HAS + s] > 0, top + jnp.log(mass), floor_value)


def row_sums(total, out, before):
    for s in range(total.shape[0]):
        mass = jnp.sum(total[s].T, axis=0, keepdims=True)
        if before is not None:
            mass = mass + before[pl.ds(s, 1), :]
        out[pl.ds(s, 1), :] = mass


def finish_rows(tab, sums, lse_ref):
    ok = jnp.ones((1, lse_ref.shape[1]), jnp.float32)
    for s in range(sums.shape[0]):
        mass = sums[pl.ds(s, 1), :]
        empty = tab[HAS + s] == 0
        fine = empty | ((mass >= sum_low) & (mass <= sum_high))
        ok = jnp.minimum(ok, jnp.where(fine, 1.0, 0.0))
        lse_ref[pl.ds(s, 1), :] = jnp.where(empty, floor_value, jnp.log(mass))
    return jnp.min(ok) > 0.5


def tile_kernel(places, base, n_in, last, tab, own, sib, *refs):
    parts, rest = refs[:n_in], refs[n_in:]
    if last:
        (sums_in, own_any, sib_any, _, _, k_out, tt, lse_ref) = rest[:8]
        tbuf, kbuf, total, sin, sk, st, sums, peak, left, right = rest[8:]
    else:
        (k_out, tt, sums_out) = rest[:3]
        tbuf, kbuf, total, sin, sk, st = rest[3:]

    def fetches(slot_local, a_src, b_src):
        return (
            pltpu.make_async_copy(a_src, tbuf.at[slot_local, pl.ds(0, ROWS_A)], sin.at[slot_local, 0]),
            pltpu.make_async_copy(b_src, tbuf.at[slot_local, pl.ds(ROWS_A, 128 - ROWS_A)], sin.at[slot_local, 1]),
        )

    for r, (a, a_base, b, b_base) in enumerate(places):
        for h in range(2):
            local = 2 * r + h
            code = tab[CODE + base + local]

            @pl.when(code >= 0)
            def _():
                for copy in fetches(local, parts[a].at[a_base + (code & 3)], parts[b].at[b_base + (code & 3)]):
                    copy.start()

    total[...] = jnp.zeros(total.shape, jnp.float32)

    def k_store(slot):
        return pltpu.make_async_copy(kbuf.at[slot - base], k_out.at[slot], sk.at[slot - base])

    def t_store(slot):
        return pltpu.make_async_copy(tbuf.at[slot - base], tt.at[slot], st.at[slot - base])

    start = tab[COUNTS] if last else 0
    stop = tab[COUNTS + 1] if last else tab[COUNTS]
    a0, b0 = parts[places[0][0]], parts[places[0][2]]

    def step(i, _):
        slot, s, _ = pair_of(tab, i)
        local = slot - base
        for copy in fetches(local, a0.at[0], b0.at[0]):
            copy.wait()
        t_store(slot).start()

        def compute(src):
            k = jnp.exp(tile_dot(src[s & 7], tbuf[local]) * inv_epsilon)
            kbuf[local] = k
            total[s] = total[s] + k

        @pl.when(s < 8)
        def _():
            compute(own)

        @pl.when(s >= 8)
        def _():
            compute(sib)

        k_store(slot).start()
        return 0

    lax.fori_loop(start, stop, step, 0)
    if last:
        row_sums(total, sums, sums_in)
        ok = finish_rows(tab, sums, lse_ref)
    else:
        row_sums(total, sums_out, None)

    def drain(i, _):
        slot = tab[LIST + i]
        k_store(slot).wait()
        t_store(slot).wait()
        return 0

    lax.fori_loop(start, stop, drain, 0)
    if last:

        @pl.when(jnp.logical_not(ok))
        def _():
            exact_rows(tab, own_any, sib_any, tt, None, left, right, total, peak, lse_ref)


def k_fetch(tab, k_in, kbuf, sin):
    def fetch(i):
        return pltpu.make_async_copy(k_in.at[tab[LIST + i]], kbuf.at[i], sin.at[i])

    lax.fori_loop(0, tab[COUNTS + 1], lambda i, c: (fetch(i).start(), c)[1], 0)
    return fetch


def row_kernel(tab, g_in, k_in, own, sib, tt, lse_ref, gbuf, vbuf, kbuf, total, peak, sums, left, right, sin):
    fetch = k_fetch(tab, k_in, kbuf, sin)
    total[...] = jnp.zeros(total.shape, jnp.float32)
    gbuf[pl.ds(0, CHIPS), :] = g_in[:, :128]
    gbuf[pl.ds(CHIPS, CHIPS), :] = g_in[:, 128:]
    scaled = gbuf[...] * inv_epsilon
    vbuf[...] = jnp.exp(scaled)
    fits = all_true((scaled >= pot_low) & (scaled <= pot_high))

    def step(i, _):
        fetch(i).wait()
        _, s, t = pair_of(tab, i)
        total[s] = total[s] + kbuf[i] * vbuf[pl.ds(t, 1), :]
        return 0

    lax.fori_loop(0, tab[COUNTS + 1], step, 0)
    row_sums(total, sums, None)
    ok = finish_rows(tab, sums, lse_ref)

    @pl.when(jnp.logical_not(ok & fits))
    def _():
        exact_rows(tab, own, sib, tt, gbuf, left, right, total, peak, lse_ref)


def column_kernel(
    tab, l0, l1, l2, l3, log_a, log_a_sib, k_in, own, sib, tt, f_ref, lse_ref, ubuf, kbuf, mass, lse, left, right, sin
):
    fetch = k_fetch(tab, k_in, kbuf, sin)
    a, b, c, d = l0[...], l1[...], l2[...], l3[...]
    top = jnp.maximum(jnp.maximum(a, c), jnp.maximum(b, d))
    summed = (jnp.exp(a - top) + jnp.exp(c - top)) + (jnp.exp(b - top) + jnp.exp(d - top))
    weights = jnp.concatenate([log_a[...], log_a_sib[...]], axis=0)
    f = epsilon * weights - epsilon * (top + jnp.log(summed))
    f_ref[...] = f[:8]
    scaled = f * inv_epsilon
    fits = all_true((scaled >= pot_low) & (scaled <= pot_high))
    u = jnp.exp(scaled)
    for s in range(ubuf.shape[0]):
        ubuf[s] = row_to_lanes(u[s : s + 1, :])
    mass[...] = jnp.full(mass.shape, -1.0, jnp.float32)

    def step(i, _):
        fetch(i).wait()
        _, s, t = pair_of(tab, i)
        mass[pl.ds(t, 1), :] = jnp.sum(kbuf[i] * ubuf[s], axis=0, keepdims=True)
        return 0

    lax.fori_loop(0, tab[COUNTS + 1], step, 0)
    m = mass[...]
    dead = m == -1.0
    ok = all_true(dead | ((m >= sum_low) & (m <= sum_high)))
    lse[...] = jnp.where(dead, floor_value, jnp.log(m))

    @pl.when(jnp.logical_not(ok & fits))
    def _():
        for s in range(ubuf.shape[0]):
            ubuf[s] = row_to_lanes(f[s : s + 1, :])

        def exact(i, _):
            slot, s, t = pair_of(tab, i)
            load_source(own, sib, s, left)
            pltpu.sync_copy(tt.at[slot], right)
            x = (ubuf[s] + tile_dot(left[...], right[...])) * inv_epsilon
            high = jnp.max(x, axis=0, keepdims=True)
            lse[pl.ds(t, 1), :] = high + jnp.log(jnp.sum(jnp.exp(x - high), axis=0, keepdims=True))
            return 0

        lax.fori_loop(0, tab[COUNTS + 1], exact, 0)

    lse_ref[:, :128] = lse[pl.ds(0, CHIPS), :]
    lse_ref[:, 128:] = lse[pl.ds(CHIPS, CHIPS), :]


def owner_kernel(parts, wanted, log_b, g_ref, back):
    halves = [parts[:, :128], parts[:, 128:]]
    asked = [jnp.broadcast_to(wanted[:, h : h + 1], halves[h].shape) for h in range(2)]
    outs = [jnp.zeros(halves[h].shape, jnp.float32) for h in range(2)]
    for j in range(g_ref.shape[0]):
        hits = [w == j for w in asked]
        top = functools.reduce(
            jnp.maximum,
            [jnp.max(jnp.where(hit, x, floor_value), axis=0, keepdims=True) for hit, x in zip(hits, halves)],
        )
        mass = sum(
            jnp.sum(jnp.where(hit, jnp.exp(x - top), 0.0), axis=0, keepdims=True) for hit, x in zip(hits, halves)
        )
        g = epsilon * log_b[pl.ds(j, 1), :] - epsilon * (top + jnp.log(mass))
        g_ref[pl.ds(j, 1), :] = g
        outs = [jnp.where(hit, g, out) for hit, out in zip(hits, outs)]
    back[:, :128] = outs[0]
    back[:, 128:] = outs[1]


def shift(value, axis, by):
    n = lax.axis_size(axis)
    return lax.ppermute(value, axis, [(i, (i + by) % n) for i in range(n)])


def round_x(block, cut):
    up, down = shift(block, "x", 1), shift(block, "x", -1)
    return up, down, shift(up[:cut], "x", 1), shift(down[cut:], "x", -1)


def round_z(block):
    cut = block.shape[0] // 2
    p1, m1 = shift(block, "z", 1), shift(block, "z", -1)
    p2, m2 = shift(p1, "z", 1), shift(m1, "z", -1)
    p3, m3 = shift(p2, "z", 1), shift(m2, "z", -1)
    return p1, m1, p2, m2, p3, m3, shift(p3[:cut], "z", 1), shift(m3[cut:], "z", -1)


def per_device(source, targets, log_a, log_b, pair_source, pair_target, pair_count):
    xi, zi, core = (lax.axis_index(a) for a in ("x", "z", "core"))
    chip = xi * ZS + zi
    local_blocks, quarter, width = targets.shape
    blocks, rows, _ = source.shape
    f32, i32 = jnp.float32, jnp.int32
    sds = jax.ShapeDtypeStruct
    params = pltpu.CompilerParams(vmem_limit_bytes=VMEM_LIMIT)

    def swap_cores(v):
        return shift(v, "core", 1)

    a_rows, b_rows = targets[:, :ROWS_A], targets[:, ROWS_A:]
    sib = swap_cores(source)
    log_a_sib = swap_cores(log_a)
    a_x = jnp.concatenate([a_rows, *round_x(a_rows, 2)])
    bz = round_z(b_rows)
    near = jnp.concatenate([b_rows, *bz[:2]])
    near_x = round_x(near, 2 * local_blocks)
    far = jnp.concatenate(bz[2:])
    far_x = round_x(far, 2 * local_blocks)
    a_z = round_z(a_x)

    order = np.arange(CHIPS)
    dz = jnp.asarray(np.array(DZ)[order // XS], i32)
    dx = jnp.asarray(np.array(DX)[order % XS], i32)
    trow = ((xi - dx) % XS) * ZS + (zi - dz) % ZS

    def own_first(two):
        return jnp.where(core == 0, two, two[::-1])

    ps = own_first(lax.dynamic_slice_in_dim(pair_source, 2 * chip, 2, 0))
    pt = own_first(lax.dynamic_slice_in_dim(pair_target, 2 * chip, 2, 0))
    cnt = own_first(lax.dynamic_slice_in_dim(pair_count, 2 * chip, 2, 0))
    live = lax.broadcasted_iota(i32, pt.shape, 1) < cnt[:, None]
    match = live[None] & (pt[None] // local_blocks == (2 * trow + core)[:, None, None])
    code = jnp.max(jnp.where(match, (ps * local_blocks + pt % local_blocks)[None], -1), axis=2).reshape(SLOTS)
    valid = code >= 0
    ids = jnp.arange(SLOTS, dtype=i32)
    rank = jnp.sum((valid[None, :] & (ids[None, :] < ids[:, None])).astype(i32), axis=1)
    listed = jnp.sum(jnp.where(valid[None, :] & (rank[None, :] == ids[:, None]), ids[None, :], 0), axis=1)
    block_of = (ids & 1) * blocks + (code >> 2)
    has = jnp.max(
        (valid[None, :] & (block_of[None, :] == jnp.arange(2 * blocks, dtype=i32)[:, None])).astype(i32), axis=1
    )
    counts = jnp.stack([jnp.sum((valid & (ids < NEAR_SLOTS)).astype(i32)), jnp.sum(valid.astype(i32))])
    tab = jnp.concatenate([code, listed, trow, has, counts, jnp.zeros((TABLE - COUNTS - 2,), i32)])

    all_live = lax.broadcasted_iota(i32, pair_target.shape, 1) < pair_count[:, None]
    asked = all_live & (pair_target // local_blocks == 2 * chip + core)
    wanted = jnp.max(jnp.where(asked, pair_target % local_blocks, -1), axis=1).reshape(CHIPS, 2)
    wanted = jnp.where(core == 0, wanted, wanted[:, ::-1])

    tiles = (SLOTS, rows, quarter)
    kept = (SLOTS, quarter, width)
    both = 2 * blocks
    exact_scratch = [pltpu.VMEM((rows, width), jnp.bfloat16), pltpu.VMEM((quarter, width), jnp.bfloat16)]
    acc = pltpu.VMEM((both, rows, quarter), f32)
    row_scratch = pltpu.VMEM((both, rows), f32)

    def tile_scratch(n):
        return [
            pltpu.VMEM((n, quarter, width), jnp.bfloat16),
            pltpu.VMEM((n, rows, quarter), f32),
            acc,
            pltpu.SemaphoreType.DMA((n, 2)),
            pltpu.SemaphoreType.DMA((n,)),
            pltpu.SemaphoreType.DMA((n,)),
        ]

    def cost(pairs):
        return pl.CostEstimate(
            flops=2 * pairs * rows * quarter * width,
            bytes_accessed=pairs * rows * quarter * 4 + both * rows * width * 2,
            transcendentals=pairs * rows * quarter,
        )

    near_in = [a_x, a_z[0], a_z[1], near, *near_x]
    near_places = []
    for j in range(NEAR):
        for k in range(XS):
            b, b_base = (3 + k, 4 * j) if k < 3 else ((6, 4 * j) if j < 2 else (7, 0))
            near_places.append((j, 4 * k, b, b_base))
    k_tiles, kept_rows, sums = pl.pallas_call(
        functools.partial(tile_kernel, near_places, 0, len(near_in), False),
        out_shape=(sds(tiles, f32), sds(kept, jnp.bfloat16), sds((both, rows), f32)),
        in_specs=[SM, VM, VM] + [ANY] * len(near_in),
        out_specs=(ANY, ANY, VM),
        scratch_shapes=tile_scratch(NEAR_SLOTS),
        compiler_params=params,
        cost_estimate=cost(12),
    )(tab, source, sib, *near_in)

    far_in = [*a_z[2:], far, *far_x]
    far_places = []
    for j in range(len(DZ) - NEAR):
        for k in range(XS):
            a, a_base = (j, 4 * k) if j < 4 else (4 + k // 2, 4 * (k % 2))
            b, b_base = (6 + k, 4 * j) if k < 3 else ((9, 4 * j) if j < 2 else (10, 4 * (j - 2)))
            far_places.append((a, a_base, b, b_base))
    n_in = len(far_in)
    k_tiles, kept_rows, part = pl.pallas_call(
        functools.partial(tile_kernel, far_places, NEAR_SLOTS, n_in, True),
        out_shape=(sds(tiles, f32), sds(kept, jnp.bfloat16), sds((both, rows), f32)),
        in_specs=[SM, VM, VM] + [ANY] * n_in + [VM, ANY, ANY, ANY, ANY],
        out_specs=(ANY, ANY, VM),
        scratch_shapes=tile_scratch(SLOTS - NEAR_SLOTS) + [row_scratch, acc, *exact_scratch],
        input_output_aliases={3 + n_in + 3: 0, 3 + n_in + 4: 1},
        compiler_params=params,
        cost_estimate=cost(20),
    )(tab, source, sib, *far_in, sums, source, sib, k_tiles, kept_rows)

    k_scratch = pltpu.VMEM(tiles, f32)
    k_sems = pltpu.SemaphoreType.DMA((SLOTS,))
    pots = pltpu.VMEM((SLOTS, quarter), f32)
    wide = (CHIPS, 2 * quarter)

    def columns(part):
        other = swap_cores(part)
        other = jnp.concatenate([other[blocks:], other[:blocks]])
        top = jnp.maximum(part, other)
        part = top + jnp.log(jnp.exp(part - top) + jnp.exp(other - top))
        parts = [part] + [shift(part, "rep", k) for k in range(1, 4)]
        return pl.pallas_call(
            column_kernel,
            out_shape=(sds((blocks, rows), f32), sds(wide, f32)),
            in_specs=[SM] + [VM] * 6 + [ANY] * 4,
            out_specs=(VM, VM),
            scratch_shapes=[acc, k_scratch, pots, pots, *exact_scratch, k_sems],
            compiler_params=params,
        )(tab, *parts, log_a, log_a_sib, k_tiles, source, sib, kept_rows)

    def swap(v):
        return lax.all_to_all(v, ("x", "z"), split_axis=0, concat_axis=0, tiled=True)

    def owner(parts):
        return pl.pallas_call(
            owner_kernel,
            out_shape=(sds((local_blocks, quarter), f32), sds(wide, f32)),
            in_specs=[VM, VM, VM],
            out_specs=(VM, VM),
        )(parts, wanted, log_b)

    f, col = columns(part)
    g, back = owner(swap(col))
    part = pl.pallas_call(
        row_kernel,
        out_shape=sds((both, rows), f32),
        in_specs=[SM, VM, ANY, ANY, ANY, ANY],
        out_specs=VM,
        scratch_shapes=[pots, pots, k_scratch, acc, acc, row_scratch, *exact_scratch, k_sems],
        compiler_params=params,
    )(tab, swap(back), k_tiles, source, sib, kept_rows)
    f, col = columns(part)
    g, _ = owner(swap(col))
    return f, g


def solution(mesh):
    fine = Mesh(mesh.devices.reshape(XS, ZS, 2, 4), ("x", "z", "core", "rep"))
    blk = ("x", "z", "core")
    in_specs = (P(blk, None, None), P(blk, "rep", None), P(blk, None), P(blk, "rep"), P(), P(), P())
    out_specs = (P(blk, None), P(blk, "rep"))
    return jax.shard_map(per_device, mesh=fine, in_specs=in_specs, out_specs=out_specs, check_vma=False)
```

```python
import functools

import jax
import jax.numpy as jnp
from jax import lax
from jax.experimental import pallas as pl
from jax.experimental.pallas import tpu as pltpu
from jax.sharding import Mesh, PartitionSpec as P

epsilon = 0.1
inv_epsilon = 10.0
floor_value = -1e30
sum_low, sum_high = 1e-13, 1e26
pot_low, pot_high = -80.0, 35.0

VM = pl.BlockSpec(memory_space=pltpu.VMEM)
SM = pl.BlockSpec(memory_space=pltpu.SMEM)
ANY = pl.BlockSpec(memory_space=pl.ANY)
MIB = 1024 * 1024

XS, ZS = 4, 8
CHIPS = XS * ZS
DZ = (0, 1, 7, 2, 6, 3, 5, 4)
DX = (0, 1, 3, 2)
GROUPS = ((0, 5), (5, 8))
SLOTS = 2 * CHIPS
CODE, LIST, TROW, SEND, HAS, COUNTS, TABLE = 0, 64, 128, 160, 208, 225, 256


def tile_dot(left, right):
    return lax.dot_general(left, right, (((1,), (1,)), ((), ())), preferred_element_type=jnp.float32)


def all_true(mask):
    return jnp.min(jnp.where(mask, 1.0, 0.0)) > 0.5


def row_to_lanes(row):
    return jnp.broadcast_to(row, (128, 128)).T


def lanes_to_row(tile):
    return jnp.sum(tile.T, axis=0, keepdims=True)


def fold(tile):
    return jnp.sum(tile.reshape(16, 8, tile.shape[1]), axis=0)


def quarters(tile):
    return [tile[:, 128 * q : 128 * (q + 1)] for q in range(4)]


def batched(start, stop, width, wait, body):
    def step(q, _):
        base = start + q * width
        for w in range(width if wait else 0):

            @pl.when(base + w < stop)
            def _():
                wait(base + w)

        for w in range(width):
            body(jnp.minimum(base + w, stop - 1), base + w < stop)
        return 0

    lax.fori_loop(0, (stop - start + width - 1) // width, step, 0)


def pair_of(tab, i):
    slot = tab[LIST + i]
    h = slot & 1
    return slot, h * 8 + (tab[CODE + slot] >> 2), h * CHIPS + tab[TROW + (slot >> 1)]


def table_kernel(named, tab):
    x, z, c = (lax.axis_index(a) for a in ("x", "z", "core"))
    for i in range(HAS, TABLE):
        tab[i] = 0
    count = 0
    for j, dz in enumerate(DZ):
        zt = (z - dz) & (ZS - 1)
        for k, dx in enumerate(DX):
            r = XS * j + k
            row = ((x - dx) & (XS - 1)) * ZS + zt
            tab[TROW + r] = row
            for h in range(2):
                code = named[2 * (x * ZS + z) + (c ^ h), 2 * row + c]
                live = code >= 0
                tab[CODE + 2 * r + h] = code
                tab[LIST + count] = 2 * r + h
                count = count + live.astype(jnp.int32)
                tab[jnp.where(live, HAS + h * 8 + (code >> 2), HAS + 16)] = 1
        for g, (_, end) in enumerate(GROUPS):
            if j + 1 == end:
                tab[COUNTS + 1 + g] = count
        for k, dx in enumerate(DX[1:]):
            far = ((x + dx) & (XS - 1)) * ZS + z
            for h in range(2):
                code = named[2 * far + (c ^ h), 2 * (x * ZS + zt) + c]
                tab[SEND + 16 * k + 2 * j + h] = jnp.where(code >= 0, code & 3, 0)


def stack_kernel(own, sib, both, sem):
    copies = [pltpu.make_async_copy(v, both.at[pl.ds(8 * i, 8)], sem.at[i]) for i, v in enumerate((own, sib))]
    for copy in copies:
        copy.start()
    for copy in copies:
        copy.wait()


def select_kernel(first, n, tab, *refs):
    blocks, outs, sem = refs[:n], refs[n : n + 3], refs[n + 3]
    copies = []
    for k in range(3):
        for j in range(n):
            for h in range(2):
                b = tab[SEND + 16 * k + 2 * (first + j) + h]
                copies.append(
                    pltpu.make_async_copy(blocks[j].at[b], outs[k].at[2 * j + h], sem.at[k, 2 * j + h])
                )
                copies[-1].start()
    for copy in copies:
        copy.wait()


def exact_rows(tab, both, kept, g_ref, total, peak, lse_ref):
    total[...] = jnp.zeros(total.shape, jnp.float32)
    peak[...] = jnp.full(peak.shape, floor_value, jnp.float32)

    def step(i, _):
        slot, s, t = pair_of(tab, i)
        x = tile_dot(kept[slot], both[s])
        if g_ref is not None:
            g = row_to_lanes(g_ref[pl.ds(t, 1), :])
            x = x + jnp.concatenate([g] * 4, axis=1)
        x = x * inv_epsilon
        high = jnp.max(x, axis=0, keepdims=True)
        mass = jnp.sum(jnp.exp(x - high), axis=0, keepdims=True)
        before = peak[pl.ds(s, 1), :]
        raised = jnp.maximum(before, high)
        total[pl.ds(s, 1), :] = total[pl.ds(s, 1), :] * jnp.exp(before - raised) + mass * jnp.exp(high - raised)
        peak[pl.ds(s, 1), :] = raised
        return 0

    lax.fori_loop(0, tab[COUNTS + len(GROUPS)], step, 0)
    for s in range(lse_ref.shape[0]):
        at = pl.ds(s, 1)
        lse_ref[at, :] = jnp.where(tab[HAS + s] > 0, peak[at, :] + jnp.log(total[at, :]), floor_value)


def finish_rows(tab, acc, before, lse_ref):
    ok = jnp.ones((1, lse_ref.shape[1]), jnp.float32)
    for s in range(acc.shape[0]):
        mass = jnp.sum(acc[s], axis=0, keepdims=True)
        if before is not None:
            mass = mass + before[pl.ds(s, 1), :]
        empty = tab[HAS + s] == 0
        fine = empty | ((mass >= sum_low) & (mass <= sum_high))
        ok = jnp.minimum(ok, jnp.where(fine, 1.0, 0.0))
        lse_ref[pl.ds(s, 1), :] = jnp.where(empty, floor_value, jnp.log(mass))
    return jnp.min(ok) > 0.5


def tile_kernel(group, tab, both, *refs):
    first, end = GROUPS[group]
    n, base = end - first, 8 * first
    last = group == len(GROUPS) - 1
    near, far, refs = refs[:n], refs[n : n + 3], refs[n + 3 :]
    if group > 0:
        sums_in, refs = refs[0], refs[3:]
    k_out, kept, sums, acc, t_sem = refs[:5]

    def fetch(slot, block):
        return pltpu.make_async_copy(block, kept.at[slot], t_sem.at[slot - base])

    for j in range(n):
        for k in range(XS):
            for h in range(2):
                local = 8 * j + 2 * k + h
                code = tab[CODE + base + local]

                @pl.when(code >= 0)
                def _():
                    block = near[j].at[code & 3] if k == 0 else far[k - 1].at[2 * j + h]
                    fetch(base + local, block).start()

    acc[...] = jnp.zeros(acc.shape, jnp.float32)

    start, stop = tab[COUNTS + group], tab[COUNTS + group + 1]

    def body(i, live):
        slot, s, _ = pair_of(tab, i)
        k = jnp.exp(tile_dot(kept[slot], both[s]) * inv_epsilon)
        k_out[slot] = k
        acc[s] = acc[s] + fold(k) * live.astype(jnp.float32)

    batched(start, stop, 2, lambda i: fetch(tab[LIST + i], near[0].at[0]).wait(), body)
    if last:
        ok = finish_rows(tab, acc, sums_in, sums)
    else:
        for s in range(acc.shape[0]):
            mass = jnp.sum(acc[s], axis=0, keepdims=True)
            sums[pl.ds(s, 1), :] = mass if group == 0 else mass + sums_in[pl.ds(s, 1), :]

    if last:
        total, peak = refs[5:]

        @pl.when(jnp.logical_not(ok))
        def _():
            exact_rows(tab, both, kept, None, total, peak, sums)


def row_kernel(tab, g_in, k_in, both, kept, lse_ref, gbuf, vbuf, acc, total, peak):
    acc[...] = jnp.zeros(acc.shape, jnp.float32)
    gbuf[pl.ds(0, CHIPS), :] = g_in[:, :128]
    gbuf[pl.ds(CHIPS, CHIPS), :] = g_in[:, 128:]
    scaled = gbuf[...] * inv_epsilon
    vbuf[...] = jnp.exp(scaled)
    fits = all_true((scaled >= pot_low) & (scaled <= pot_high))

    def body(i, live):
        slot, s, t = pair_of(tab, i)
        v = row_to_lanes(vbuf[pl.ds(t, 1), :] * live.astype(jnp.float32))
        part = [fold(k * v) for k in quarters(k_in.at[slot])]
        acc[s] = acc[s] + jnp.concatenate(part, axis=1)

    batched(0, tab[COUNTS + len(GROUPS)], 4, None, body)
    ok = finish_rows(tab, acc, None, lse_ref)

    @pl.when(jnp.logical_not(ok & fits))
    def _():
        exact_rows(tab, both, kept, gbuf, total, peak, lse_ref)


def column_kernel(
    tab, l0, l1, l2, l3, log_a, log_a_sib, k_in, both, kept, f_ref, lse_ref, ubuf, mass, lse
):
    a, b, c, d = l0[...], l1[...], l2[...], l3[...]
    top = jnp.maximum(jnp.maximum(a, c), jnp.maximum(b, d))
    summed = (jnp.exp(a - top) + jnp.exp(c - top)) + (jnp.exp(b - top) + jnp.exp(d - top))
    weights = jnp.concatenate([log_a[...], log_a_sib[...]], axis=0)
    f = epsilon * weights - epsilon * (top + jnp.log(summed))
    f_ref[...] = f[:8]
    scaled = f * inv_epsilon
    fits = all_true((scaled >= pot_low) & (scaled <= pot_high))
    ubuf[...] = jnp.exp(scaled)
    mass[...] = jnp.full(mass.shape, -1.0, jnp.float32)

    def body(i, live):
        slot, s, t = pair_of(tab, i)
        us = quarters(ubuf[pl.ds(s, 1), :])
        ks = quarters(k_in.at[slot])
        part = (ks[0] * us[0] + ks[1] * us[1]) + (ks[2] * us[2] + ks[3] * us[3])
        mass[pl.ds(t, 1), :] = lanes_to_row(part)

    batched(0, tab[COUNTS + len(GROUPS)], 4, None, body)
    m = mass[...]
    dead = m == -1.0
    ok = all_true(dead | ((m >= sum_low) & (m <= sum_high)))
    lse[...] = jnp.where(dead, floor_value, jnp.log(m))

    @pl.when(jnp.logical_not(ok & fits))
    def _():
        ubuf[...] = f

        def exact(i, _):
            slot, s, t = pair_of(tab, i)
            x = (ubuf[pl.ds(s, 1), :] + tile_dot(kept[slot], both[s])) * inv_epsilon
            high = jnp.max(x, axis=1, keepdims=True)
            column = high + jnp.log(jnp.sum(jnp.exp(x - high), axis=1, keepdims=True))
            lse[pl.ds(t, 1), :] = jnp.broadcast_to(column, (128, 128)).T[:1, :]
            return 0

        lax.fori_loop(0, tab[COUNTS + len(GROUPS)], exact, 0)

    lse_ref[:, :128] = lse[pl.ds(0, CHIPS), :]
    lse_ref[:, 128:] = lse[pl.ds(CHIPS, CHIPS), :]


def owner_kernel(parts, wanted, log_b, g_ref, back):
    halves = [parts[:, :128], parts[:, 128:]]
    asked = [jnp.broadcast_to(wanted[:, h : h + 1], halves[h].shape) for h in range(2)]
    outs = [jnp.zeros(halves[h].shape, jnp.float32) for h in range(2)]
    for j in range(g_ref.shape[0]):
        hits = [w == j for w in asked]
        top = functools.reduce(
            jnp.maximum,
            [jnp.max(jnp.where(hit, x, floor_value), axis=0, keepdims=True) for hit, x in zip(hits, halves)],
        )
        mass = sum(
            jnp.sum(jnp.where(hit, jnp.exp(x - top), 0.0), axis=0, keepdims=True) for hit, x in zip(hits, halves)
        )
        g = epsilon * log_b[pl.ds(j, 1), :] - epsilon * (top + jnp.log(mass))
        g_ref[pl.ds(j, 1), :] = g
        outs = [jnp.where(hit, g, out) for hit, out in zip(hits, outs)]
    back[:, :128] = outs[0]
    back[:, 128:] = outs[1]


def shift(value, axis, by):
    n = lax.axis_size(axis)
    return lax.ppermute(value, axis, [(i, (i + by) % n) for i in range(n)])


def per_device(source, targets, log_a, log_b, pair_source, pair_target, pair_count):
    xi, zi, core = (lax.axis_index(a) for a in ("x", "z", "core"))
    local_blocks, quarter, width = targets.shape
    blocks, rows, _ = source.shape
    f32, i32, bf16 = jnp.float32, jnp.int32, jnp.bfloat16
    sds = jax.ShapeDtypeStruct

    def params(mib):
        return pltpu.CompilerParams(vmem_limit_bytes=mib * MIB)

    pin = pltpu.with_memory_space_constraint

    def swap_cores(v):
        return shift(v, "core", 1)

    owners = pair_target.shape[0]
    live = lax.broadcasted_iota(i32, pair_target.shape, 1) < pair_count[:, None]
    match = live[:, None, :] & ((pair_target // local_blocks)[:, None, :] == jnp.arange(owners, dtype=i32)[None, :, None])
    named = jnp.max(jnp.where(match, (pair_source * local_blocks + pair_target % local_blocks)[:, None, :], -1), axis=2)
    tab = pl.pallas_call(table_kernel, out_shape=sds((TABLE,), i32), in_specs=[SM], out_specs=SM)(named)
    tab = pin(tab, pltpu.HBM)
    wanted = lax.dynamic_index_in_dim(named, 2 * (xi * ZS + zi) + core, 1, keepdims=False).reshape(CHIPS, 2)
    wanted = jnp.where(core == 0, wanted, wanted[:, ::-1])
    wanted = jnp.where(wanted >= 0, wanted & 3, -1)

    sib = swap_cores(source)
    log_a_sib = swap_cores(log_a)
    p1, m1 = shift(targets, "z", 1), shift(targets, "z", -1)
    p1, m1, tab = lax.optimization_barrier((p1, m1, tab))
    p2, m2 = shift(p1, "z", 1), shift(m1, "z", -1)
    p3, m3 = shift(p2, "z", 1), shift(m2, "z", -1)
    p4 = shift(p3, "z", 1)
    held = [[pin(v, pltpu.VMEM) for v in group] for group in ((targets, p1, m1, p2, m2), (p3, m3, p4))]

    def along_x(group, after):
        first, end = GROUPS[group]
        n = end - first
        sent = pl.pallas_call(
            functools.partial(select_kernel, first, n),
            out_shape=(pltpu.VMEM((2 * n, quarter, width), bf16),) * 3,
            in_specs=[SM] + [ANY] * n,
            out_specs=(ANY,) * 3,
            scratch_shapes=[pltpu.SemaphoreType.DMA((3, 2 * n))],
            compiler_params=params(4),
        )(tab, *held[group])
        if after is not None:
            held_back = lax.optimization_barrier((*sent, *after))
            sent, after = held_back[:3], held_back[3:]
        return [pin(shift(v, "x", dx), pltpu.VMEM) for v, dx in zip(sent, DX[1:])], after

    tiles = (SLOTS, quarter, rows)
    kept = (SLOTS, quarter, width)
    both = 2 * blocks
    row_scratch = [pltpu.VMEM((both, rows), f32)] * 2
    acc = pltpu.VMEM((both, 8, rows), f32)

    sources = pl.pallas_call(
        stack_kernel,
        out_shape=pltpu.VMEM((both, rows, width), bf16),
        in_specs=[ANY, ANY],
        out_specs=VM,
        scratch_shapes=[pltpu.SemaphoreType.DMA((2,))],
        compiler_params=params(1),
    )(pin(source, pltpu.HBM), sib)

    def tile_call(group, far, before):
        first, end = GROUPS[group]
        slots = 8 * (end - first)
        ins = [tab, pin(sources, pltpu.VMEM), *held[group], *far]
        specs = [SM, VM] + [ANY] * (len(ins) - 2)
        alias = {}
        if before:
            k_tiles, kept_rows, sums = before
            ins += [sums, pin(k_tiles, pltpu.VMEM), pin(kept_rows, pltpu.VMEM)]
            specs += [VM, VM, VM]
            alias = {len(ins) - 2: 0, len(ins) - 1: 1}
        scratch = [acc, pltpu.SemaphoreType.DMA((slots,))]
        if group == len(GROUPS) - 1:
            scratch += row_scratch
        return pl.pallas_call(
            functools.partial(tile_kernel, group),
            out_shape=(pltpu.VMEM(tiles, f32), pltpu.VMEM(kept, bf16), sds((both, rows), f32)),
            in_specs=specs,
            out_specs=(VM, VM, VM),
            scratch_shapes=scratch,
            input_output_aliases=alias,
            compiler_params=params(4),
            cost_estimate=pl.CostEstimate(
                flops=slots * rows * quarter * width, bytes_accessed=10 * MIB, transcendentals=slots * rows * quarter // 2
            ),
        )(*ins)

    near, _ = along_x(0, None)
    far, (wanted, log_a_sib) = along_x(1, (wanted, log_a_sib))
    k_tiles, kept_rows, part = tile_call(1, far, tile_call(0, near, None))

    resident = [pin(v, pltpu.VMEM) for v in (k_tiles, sources, kept_rows)]
    pots = pltpu.VMEM((SLOTS, quarter), f32)
    wide = (CHIPS, 2 * quarter)

    def columns(part):
        other = swap_cores(part)
        other = jnp.concatenate([other[blocks:], other[:blocks]])
        top = jnp.maximum(part, other)
        part = top + jnp.log(jnp.exp(part - top) + jnp.exp(other - top))
        parts = [part] + [shift(part, "rep", k) for k in range(1, 4)]
        return pl.pallas_call(
            column_kernel,
            out_shape=(sds((blocks, rows), f32), sds(wide, f32)),
            in_specs=[SM] + [VM] * 9,
            out_specs=(VM, VM),
            scratch_shapes=[row_scratch[0], pots, pots],
            compiler_params=params(4),
        )(tab, *parts, log_a, log_a_sib, *resident)

    def swap(v):
        return lax.all_to_all(v, ("x", "z"), split_axis=0, concat_axis=0, tiled=True)

    def owner(parts):
        return pl.pallas_call(
            owner_kernel,
            out_shape=(sds((local_blocks, quarter), f32), sds(wide, f32)),
            in_specs=[VM, VM, VM],
            out_specs=(VM, VM),
            compiler_params=params(4),
        )(parts, wanted, log_b)

    f, col = columns(part)
    g, back = owner(swap(col))
    part = pl.pallas_call(
        row_kernel,
        out_shape=sds((both, rows), f32),
        in_specs=[SM] + [VM] * 4,
        out_specs=VM,
        scratch_shapes=[pots, pots, acc, *row_scratch],
        compiler_params=params(4),
    )(tab, swap(back), *resident)
    f, col = columns(part)
    g, _ = owner(swap(col))
    return f, g


def solution(mesh):
    fine = Mesh(mesh.devices.reshape(XS, ZS, 2, 4), ("x", "z", "core", "rep"))
    blk = ("x", "z", "core")
    in_specs = (P(blk, None, None), P(blk, "rep", None), P(blk, None), P(blk, "rep"), P(), P(), P())
    out_specs = (P(blk, None), P(blk, "rep"))
    return jax.shard_map(per_device, mesh=fine, in_specs=in_specs, out_specs=out_specs, check_vma=False)
```

```python
import functools

import jax
import jax.numpy as jnp
from jax import lax
from jax.experimental import pallas as pl
from jax.experimental.pallas import tpu as pltpu
from jax.sharding import Mesh, PartitionSpec as P

epsilon = 0.1
inv_epsilon = 10.0
floor_value = -1e30
sum_low, sum_high = 1e-13, 1e26
pot_low, pot_high = -80.0, 35.0

VM = pl.BlockSpec(memory_space=pltpu.VMEM)
SM = pl.BlockSpec(memory_space=pltpu.SMEM)
ANY = pl.BlockSpec(memory_space=pl.ANY)
MIB = 1024 * 1024

XS, ZS = 4, 8
CHIPS = XS * ZS
DZ = (0, 1, 7, 2, 6, 3, 5, 4)
DX = (0, 1, 3, 2)
GROUPS = ((0, 1), (1, 5), (5, 8))
TILES = ((0, 2), (2, 3))


def rows_of(group, k):
    if k == XS - 1 and group < 2:
        return ((0, 0), (0, GROUPS[1][1]))[group]
    return GROUPS[group]


PARTS = [(g, k) for g in range(len(GROUPS)) for k in range(XS) if rows_of(g, k)[0] < rows_of(g, k)[1]]
SLOTS = 2 * CHIPS
CODE, LIST, TROW, SEND, HAS, COUNTS, TABLE = 0, 64, 128, 160, 224, 241, 256


def tile_dot(left, right):
    return lax.dot_general(left, right, (((1,), (1,)), ((), ())), preferred_element_type=jnp.float32)


def all_true(mask):
    return jnp.min(jnp.where(mask, 1.0, 0.0)) > 0.5


def row_to_lanes(row):
    return jnp.broadcast_to(row, (128, 128)).T


def lanes_to_row(tile):
    return jnp.sum(tile.T, axis=0, keepdims=True)


def fold(tile):
    return jnp.sum(tile.reshape(16, 8, tile.shape[1]), axis=0)


def quarters(tile):
    return [tile[:, 128 * q : 128 * (q + 1)] for q in range(4)]


def batched(start, stop, width, wait, body):
    def step(q, _):
        base = start + q * width
        for w in range(width if wait else 0):

            @pl.when(base + w < stop)
            def _():
                wait(base + w)

        for w in range(width):
            body(jnp.minimum(base + w, stop - 1), base + w < stop)
        return 0

    lax.fori_loop(0, (stop - start + width - 1) // width, step, 0)


def pair_of(tab, i):
    slot = tab[LIST + i]
    h = slot & 1
    return slot, h * 8 + (tab[CODE + slot] >> 2), h * CHIPS + tab[TROW + (slot >> 1)]


def table_kernel(named, tab):
    x, z, c = (lax.axis_index(a) for a in ("x", "z", "core"))
    for i in range(HAS, TABLE):
        tab[i] = 0
    count = 0
    for j, dz in enumerate(DZ):
        zt = (z - dz) & (ZS - 1)
        for k, dx in enumerate(DX):
            r = XS * j + k
            row = ((x - dx) & (XS - 1)) * ZS + zt
            tab[TROW + r] = row
            for h in range(2):
                code = named[2 * (x * ZS + z) + (c ^ h), 2 * row + c]
                live = code >= 0
                tab[CODE + 2 * r + h] = code
                tab[LIST + count] = 2 * r + h
                count = count + live.astype(jnp.int32)
                tab[jnp.where(live, HAS + h * 8 + (code >> 2), HAS + 16)] = 1
        for g, (_, end) in enumerate(TILES):
            if j + 1 == GROUPS[end - 1][1]:
                tab[COUNTS + 1 + g] = count
        for k, dx in enumerate(DX):
            far = ((x + dx) & (XS - 1)) * ZS + z
            for h in range(2):
                code = named[2 * far + (c ^ h), 2 * (x * ZS + zt) + c]
                tab[SEND + 16 * k + 2 * j + h] = jnp.where(code >= 0, code & 3, 0)


def stack_kernel(own, sib, both, sem):
    copies = [pltpu.make_async_copy(v, both.at[pl.ds(8 * i, 8)], sem.at[i]) for i, v in enumerate((own, sib))]
    for copy in copies:
        copy.start()
    for copy in copies:
        copy.wait()


def select_kernel(group, n, tab, *refs):
    blocks, outs, sem = refs[:n], refs[n:-1], refs[-1]
    base = GROUPS[group][1] - n
    copies = []
    for out, k in zip(outs, [k for g, k in PARTS if g == group]):
        low, high = rows_of(group, k)
        for j in range(low, high):
            for h in range(2):
                i = 2 * (j - low) + h
                b = tab[SEND + 16 * k + 2 * j + h]
                copies.append(pltpu.make_async_copy(blocks[j - base].at[b], out.at[i], sem.at[k, i]))
                copies[-1].start()
    for copy in copies:
        copy.wait()


def exact_rows(tab, both, kept, g_ref, total, peak, lse_ref):
    total[...] = jnp.zeros(total.shape, jnp.float32)
    peak[...] = jnp.full(peak.shape, floor_value, jnp.float32)

    def step(i, _):
        slot, s, t = pair_of(tab, i)
        x = tile_dot(kept[slot], both[s])
        if g_ref is not None:
            g = row_to_lanes(g_ref[pl.ds(t, 1), :])
            x = x + jnp.concatenate([g] * 4, axis=1)
        x = x * inv_epsilon
        high = jnp.max(x, axis=0, keepdims=True)
        mass = jnp.sum(jnp.exp(x - high), axis=0, keepdims=True)
        before = peak[pl.ds(s, 1), :]
        raised = jnp.maximum(before, high)
        total[pl.ds(s, 1), :] = total[pl.ds(s, 1), :] * jnp.exp(before - raised) + mass * jnp.exp(high - raised)
        peak[pl.ds(s, 1), :] = raised
        return 0

    lax.fori_loop(0, tab[COUNTS + len(TILES)], step, 0)
    for s in range(lse_ref.shape[0]):
        at = pl.ds(s, 1)
        lse_ref[at, :] = jnp.where(tab[HAS + s] > 0, peak[at, :] + jnp.log(total[at, :]), floor_value)


def finish_rows(tab, acc, before, lse_ref):
    ok = jnp.ones((1, lse_ref.shape[1]), jnp.float32)
    for s in range(acc.shape[0]):
        mass = jnp.sum(acc[s], axis=0, keepdims=True)
        if before is not None:
            mass = mass + before[pl.ds(s, 1), :]
        empty = tab[HAS + s] == 0
        fine = empty | ((mass >= sum_low) & (mass <= sum_high))
        ok = jnp.minimum(ok, jnp.where(fine, 1.0, 0.0))
        lse_ref[pl.ds(s, 1), :] = jnp.where(empty, floor_value, jnp.log(mass))
    return jnp.min(ok) > 0.5


def tile_kernel(group, tab, both, *refs):
    groups = GROUPS[slice(*TILES[group])]
    first, end = groups[0][0], groups[-1][1]
    n, base = end - first, 8 * first
    last = group == len(TILES) - 1
    here = [(g, k) for g, k in PARTS if GROUPS[g] in groups]
    parts, refs = refs[: len(here)], refs[len(here) :]
    if group > 0:
        sums_in, refs = refs[0], refs[3:]
    k_out, kept, sums, acc, t_sem = refs[:5]

    def fetch(slot, block):
        return pltpu.make_async_copy(block, kept.at[slot], t_sem.at[slot - base])

    for part, (g, k) in zip(parts, here):
        low, high = rows_of(g, k)
        for j in range(low, high):
            for h in range(2):
                slot = 8 * j + 2 * k + h

                @pl.when(tab[CODE + slot] >= 0)
                def _():
                    fetch(slot, part.at[2 * (j - low) + h]).start()

    acc[...] = jnp.zeros(acc.shape, jnp.float32)

    start, stop = tab[COUNTS + group], tab[COUNTS + group + 1]

    def body(i, live):
        slot, s, _ = pair_of(tab, i)
        k = jnp.exp(tile_dot(kept[slot], both[s]) * inv_epsilon)
        k_out[slot] = k
        acc[s] = acc[s] + fold(k) * live.astype(jnp.float32)

    batched(start, stop, 2, lambda i: fetch(tab[LIST + i], parts[0].at[0]).wait(), body)
    if last:
        ok = finish_rows(tab, acc, sums_in, sums)
    else:
        for s in range(acc.shape[0]):
            mass = jnp.sum(acc[s], axis=0, keepdims=True)
            sums[pl.ds(s, 1), :] = mass if group == 0 else mass + sums_in[pl.ds(s, 1), :]

    if last:
        total, peak = refs[5:]

        @pl.when(jnp.logical_not(ok))
        def _():
            exact_rows(tab, both, kept, None, total, peak, sums)


def row_kernel(tab, g_in, k_in, both, kept, lse_ref, gbuf, vbuf, acc, total, peak):
    acc[...] = jnp.zeros(acc.shape, jnp.float32)
    gbuf[pl.ds(0, CHIPS), :] = g_in[:, :128]
    gbuf[pl.ds(CHIPS, CHIPS), :] = g_in[:, 128:]
    scaled = gbuf[...] * inv_epsilon
    vbuf[...] = jnp.exp(scaled)
    fits = all_true((scaled >= pot_low) & (scaled <= pot_high))

    def body(i, live):
        slot, s, t = pair_of(tab, i)
        v = row_to_lanes(vbuf[pl.ds(t, 1), :] * live.astype(jnp.float32))
        part = [fold(k * v) for k in quarters(k_in.at[slot])]
        acc[s] = acc[s] + jnp.concatenate(part, axis=1)

    batched(0, tab[COUNTS + len(TILES)], 4, None, body)
    ok = finish_rows(tab, acc, None, lse_ref)

    @pl.when(jnp.logical_not(ok & fits))
    def _():
        exact_rows(tab, both, kept, gbuf, total, peak, lse_ref)


def column_kernel(
    tab, l0, l1, l2, l3, log_a, log_a_sib, k_in, both, kept, f_ref, lse_ref, ubuf, mass, lse
):
    a, b, c, d = l0[...], l1[...], l2[...], l3[...]
    top = jnp.maximum(jnp.maximum(a, c), jnp.maximum(b, d))
    summed = (jnp.exp(a - top) + jnp.exp(c - top)) + (jnp.exp(b - top) + jnp.exp(d - top))
    weights = jnp.concatenate([log_a[...], log_a_sib[...]], axis=0)
    f = epsilon * weights - epsilon * (top + jnp.log(summed))
    f_ref[...] = f[:8]
    scaled = f * inv_epsilon
    fits = all_true((scaled >= pot_low) & (scaled <= pot_high))
    ubuf[...] = jnp.exp(scaled)
    mass[...] = jnp.full(mass.shape, -1.0, jnp.float32)

    def body(i, live):
        slot, s, t = pair_of(tab, i)
        us = quarters(ubuf[pl.ds(s, 1), :])
        ks = quarters(k_in.at[slot])
        part = (ks[0] * us[0] + ks[1] * us[1]) + (ks[2] * us[2] + ks[3] * us[3])
        mass[pl.ds(t, 1), :] = lanes_to_row(part)

    batched(0, tab[COUNTS + len(TILES)], 4, None, body)
    m = mass[...]
    dead = m == -1.0
    ok = all_true(dead | ((m >= sum_low) & (m <= sum_high)))
    lse[...] = jnp.where(dead, floor_value, jnp.log(m))

    @pl.when(jnp.logical_not(ok & fits))
    def _():
        ubuf[...] = f

        def exact(i, _):
            slot, s, t = pair_of(tab, i)
            x = (ubuf[pl.ds(s, 1), :] + tile_dot(kept[slot], both[s])) * inv_epsilon
            high = jnp.max(x, axis=1, keepdims=True)
            column = high + jnp.log(jnp.sum(jnp.exp(x - high), axis=1, keepdims=True))
            lse[pl.ds(t, 1), :] = jnp.broadcast_to(column, (128, 128)).T[:1, :]
            return 0

        lax.fori_loop(0, tab[COUNTS + len(TILES)], exact, 0)

    lse_ref[:, :128] = lse[pl.ds(0, CHIPS), :]
    lse_ref[:, 128:] = lse[pl.ds(CHIPS, CHIPS), :]


def owner_kernel(parts, wanted, log_b, g_ref, back):
    halves = [parts[:, :128], parts[:, 128:]]
    asked = [jnp.broadcast_to(wanted[:, h : h + 1], halves[h].shape) for h in range(2)]
    outs = [jnp.zeros(halves[h].shape, jnp.float32) for h in range(2)]
    for j in range(g_ref.shape[0]):
        hits = [w == j for w in asked]
        top = functools.reduce(
            jnp.maximum,
            [jnp.max(jnp.where(hit, x, floor_value), axis=0, keepdims=True) for hit, x in zip(hits, halves)],
        )
        mass = sum(
            jnp.sum(jnp.where(hit, jnp.exp(x - top), 0.0), axis=0, keepdims=True) for hit, x in zip(hits, halves)
        )
        g = epsilon * log_b[pl.ds(j, 1), :] - epsilon * (top + jnp.log(mass))
        g_ref[pl.ds(j, 1), :] = g
        outs = [jnp.where(hit, g, out) for hit, out in zip(hits, outs)]
    back[:, :128] = outs[0]
    back[:, 128:] = outs[1]


def shift(value, axis, by):
    n = lax.axis_size(axis)
    return lax.ppermute(value, axis, [(i, (i + by) % n) for i in range(n)])


def per_device(source, targets, log_a, log_b, pair_source, pair_target, pair_count):
    xi, zi, core = (lax.axis_index(a) for a in ("x", "z", "core"))
    local_blocks, quarter, width = targets.shape
    blocks, rows, _ = source.shape
    f32, i32, bf16 = jnp.float32, jnp.int32, jnp.bfloat16
    sds = jax.ShapeDtypeStruct

    def params(mib):
        return pltpu.CompilerParams(vmem_limit_bytes=mib * MIB)

    pin = pltpu.with_memory_space_constraint

    def swap_cores(v):
        return shift(v, "core", 1)

    owners = pair_target.shape[0]
    live = lax.broadcasted_iota(i32, pair_target.shape, 1) < pair_count[:, None]
    match = live[:, None, :] & ((pair_target // local_blocks)[:, None, :] == jnp.arange(owners, dtype=i32)[None, :, None])
    named = jnp.max(jnp.where(match, (pair_source * local_blocks + pair_target % local_blocks)[:, None, :], -1), axis=2)
    tab = pl.pallas_call(table_kernel, out_shape=sds((TABLE,), i32), in_specs=[SM], out_specs=SM)(named)
    tab = pin(tab, pltpu.HBM)
    wanted = lax.dynamic_index_in_dim(named, 2 * (xi * ZS + zi) + core, 1, keepdims=False).reshape(CHIPS, 2)
    wanted = jnp.where(core == 0, wanted, wanted[:, ::-1])
    wanted = jnp.where(wanted >= 0, wanted & 3, -1)

    sib = swap_cores(source)
    log_a_sib = swap_cores(log_a)
    p1, m1 = shift(targets, "z", 1), shift(targets, "z", -1)
    p1, m1, tab = lax.optimization_barrier((p1, m1, tab))
    p2, m2 = shift(p1, "z", 1), shift(m1, "z", -1)

    def select(group, *blocks):
        n = len(blocks)
        spans = [rows_of(group, k) for g, k in PARTS if g == group]
        return pl.pallas_call(
            functools.partial(select_kernel, group, n),
            out_shape=[pltpu.VMEM((2 * (high - low), quarter, width), bf16) for low, high in spans],
            in_specs=[SM] + [ANY] * n,
            out_specs=[ANY] * len(spans),
            scratch_shapes=[pltpu.SemaphoreType.DMA((XS, 10))],
            compiler_params=params(4),
        )(tab, *[pin(v, pltpu.VMEM) for v in blocks])

    def along_x(blocks):
        return [blocks[0], *[shift(v, "x", dx) for v, dx in zip(blocks[1:], DX[1:])]]

    first = along_x(select(0, targets))
    p3, m3 = shift(p2, "z", 1), shift(m2, "z", -1)
    p4 = shift(p3, "z", 1)
    second = select(1, targets, p1, m1, p2, m2)
    second, first = lax.optimization_barrier((second, first))
    second = along_x(second)
    third = along_x(select(2, p3, m3, p4))
    held = [first, *[[pin(v, pltpu.VMEM) for v in group] for group in (second, third)]]

    tiles = (SLOTS, quarter, rows)
    kept = (SLOTS, quarter, width)
    both = 2 * blocks
    row_scratch = [pltpu.VMEM((both, rows), f32)] * 2
    acc = pltpu.VMEM((both, 8, rows), f32)

    sources = pl.pallas_call(
        stack_kernel,
        out_shape=pltpu.VMEM((both, rows, width), bf16),
        in_specs=[ANY, ANY],
        out_specs=VM,
        scratch_shapes=[pltpu.SemaphoreType.DMA((2,))],
        compiler_params=params(1),
    )(pin(source, pltpu.HBM), sib)

    def tile_call(group, before):
        groups = slice(*TILES[group])
        first, end = GROUPS[groups][0][0], GROUPS[groups][-1][1]
        slots = 8 * (end - first)
        ins = [tab, pin(sources, pltpu.VMEM), *sum(held[groups], [])]
        specs = [SM, VM] + [ANY] * (len(ins) - 2)
        alias = {}
        if before:
            k_tiles, kept_rows, sums = before
            ins += [sums, pin(k_tiles, pltpu.VMEM), pin(kept_rows, pltpu.VMEM)]
            specs += [VM, VM, VM]
            alias = {len(ins) - 2: 0, len(ins) - 1: 1}
        scratch = [acc, pltpu.SemaphoreType.DMA((slots,))]
        if group == len(TILES) - 1:
            scratch += row_scratch
        return pl.pallas_call(
            functools.partial(tile_kernel, group),
            out_shape=(pltpu.VMEM(tiles, f32), pltpu.VMEM(kept, bf16), sds((both, rows), f32)),
            in_specs=specs,
            out_specs=(VM, VM, VM),
            scratch_shapes=scratch,
            input_output_aliases=alias,
            compiler_params=params(4),
            cost_estimate=pl.CostEstimate(
                flops=slots * rows * quarter * width, bytes_accessed=10 * MIB, transcendentals=slots * rows * quarter // 2
            ),
        )(*ins)

    k_tiles, kept_rows, sums = tile_call(0, None)
    sums, wanted, log_a_sib = lax.optimization_barrier((sums, wanted, log_a_sib))
    k_tiles, kept_rows, part = tile_call(1, (k_tiles, kept_rows, sums))

    resident = [pin(v, pltpu.VMEM) for v in (k_tiles, sources, kept_rows)]
    pots = pltpu.VMEM((SLOTS, quarter), f32)
    wide = (CHIPS, 2 * quarter)

    def columns(part):
        other = swap_cores(part)
        other = jnp.concatenate([other[blocks:], other[:blocks]])
        top = jnp.maximum(part, other)
        part = top + jnp.log(jnp.exp(part - top) + jnp.exp(other - top))
        parts = [part] + [shift(part, "rep", k) for k in range(1, 4)]
        return pl.pallas_call(
            column_kernel,
            out_shape=(sds((blocks, rows), f32), sds(wide, f32)),
            in_specs=[SM] + [VM] * 9,
            out_specs=(VM, VM),
            scratch_shapes=[row_scratch[0], pots, pots],
            compiler_params=params(4),
        )(tab, *parts, log_a, log_a_sib, *resident)

    def swap(v):
        return lax.all_to_all(v, ("x", "z"), split_axis=0, concat_axis=0, tiled=True)

    def owner(parts):
        return pl.pallas_call(
            owner_kernel,
            out_shape=(sds((local_blocks, quarter), f32), sds(wide, f32)),
            in_specs=[VM, VM, VM],
            out_specs=(VM, VM),
            compiler_params=params(4),
        )(parts, wanted, log_b)

    f, col = columns(part)
    g, back = owner(swap(col))
    part = pl.pallas_call(
        row_kernel,
        out_shape=sds((both, rows), f32),
        in_specs=[SM] + [VM] * 4,
        out_specs=VM,
        scratch_shapes=[pots, pots, acc, *row_scratch],
        compiler_params=params(4),
    )(tab, swap(back), *resident)
    f, col = columns(part)
    g, _ = owner(swap(col))
    return f, g


def solution(mesh):
    fine = Mesh(mesh.devices.reshape(XS, ZS, 2, 4), ("x", "z", "core", "rep"))
    blk = ("x", "z", "core")
    in_specs = (P(blk, None, None), P(blk, "rep", None), P(blk, None), P(blk, "rep"), P(), P(), P())
    out_specs = (P(blk, None), P(blk, "rep"))
    return jax.shard_map(per_device, mesh=fine, in_specs=in_specs, out_specs=out_specs, check_vma=False)
```

```python
import functools

import jax
import jax.numpy as jnp
from jax import lax
from jax.experimental import pallas as pl
from jax.experimental.pallas import tpu as pltpu
from jax.sharding import Mesh, PartitionSpec as P

epsilon = 0.1
inv_epsilon = 10.0
floor_value = -1e30
sum_low, sum_high = 1e-13, 1e26
pot_low, pot_high = -80.0, 35.0

VM = pl.BlockSpec(memory_space=pltpu.VMEM)
SM = pl.BlockSpec(memory_space=pltpu.SMEM)
ANY = pl.BlockSpec(memory_space=pl.ANY)
MIB = 1024 * 1024

XS, ZS = 4, 8
CHIPS = XS * ZS
DZ = (0, 1, 7, 2, 6, 3, 5, 4)
DX = (0, 1, 3, 2)
GROUPS = ((0, 1), (1, 5), (5, 8))


def rows_of(group, k):
    if k == 0:
        return ((0, 0), (0, 0), (0, len(DZ)))[group]
    if k == XS - 1 and group < 2:
        return ((0, 0), (0, GROUPS[1][1]))[group]
    return GROUPS[group]


PARTS = [(g, k) for g in range(len(GROUPS)) for k in range(XS) if rows_of(g, k)[0] < rows_of(g, k)[1]]
TILES = (
    [(j, k) for j in range(len(DZ)) for k in range(XS) if j < GROUPS[2][0] or k == 0],
    [(j, k) for j in range(*GROUPS[2]) for k in range(1, XS)],
)


def parts_of(group):
    return [(g, k) for g, k in PARTS if any((j, k) in TILES[group] for j in range(*rows_of(g, k)))]


SLOTS = 2 * CHIPS
CODE, LIST, TROW, SEND, HAS, COUNTS, TABLE = 0, 64, 128, 160, 224, 241, 256


def tile_dot(left, right):
    return lax.dot_general(left, right, (((1,), (1,)), ((), ())), preferred_element_type=jnp.float32)


def all_true(mask):
    return jnp.min(jnp.where(mask, 1.0, 0.0)) > 0.5


def row_to_lanes(row):
    return jnp.broadcast_to(row, (128, 128)).T


def lanes_to_row(tile):
    return jnp.sum(tile.T, axis=0, keepdims=True)


def fold(tile):
    return jnp.sum(tile.reshape(16, 8, tile.shape[1]), axis=0)


def quarters(tile):
    return [tile[:, 128 * q : 128 * (q + 1)] for q in range(4)]


def batched(start, stop, width, wait, body):
    def step(q, _):
        base = start + q * width
        for w in range(width if wait else 0):

            @pl.when(base + w < stop)
            def _():
                wait(base + w)

        for w in range(width):
            body(jnp.minimum(base + w, stop - 1), base + w < stop)
        return 0

    lax.fori_loop(0, (stop - start + width - 1) // width, step, 0)


def pair_of(tab, i):
    slot = tab[LIST + i]
    h = slot & 1
    return slot, h * 8 + (tab[CODE + slot] >> 2), h * CHIPS + tab[TROW + (slot >> 1)]


def table_kernel(named, tab):
    x, z, c = (lax.axis_index(a) for a in ("x", "z", "core"))
    for i in range(HAS, TABLE):
        tab[i] = 0
    count = 0
    for group in range(len(TILES)):
        for j, k in TILES[group]:
            r = XS * j + k
            row = ((x - DX[k]) & (XS - 1)) * ZS + ((z - DZ[j]) & (ZS - 1))
            tab[TROW + r] = row
            for h in range(2):
                code = named[2 * (x * ZS + z) + (c ^ h), 2 * row + c]
                live = code >= 0
                tab[CODE + 2 * r + h] = code
                tab[LIST + count] = 2 * r + h
                count = count + live.astype(jnp.int32)
                tab[jnp.where(live, HAS + h * 8 + (code >> 2), HAS + 16)] = 1
        tab[COUNTS + 1 + group] = count
    for j, dz in enumerate(DZ):
        zt = (z - dz) & (ZS - 1)
        for k, dx in enumerate(DX):
            far = ((x + dx) & (XS - 1)) * ZS + z
            for h in range(2):
                code = named[2 * far + (c ^ h), 2 * (x * ZS + zt) + c]
                tab[SEND + 16 * k + 2 * j + h] = jnp.where(code >= 0, code & 3, 0)


def stack_kernel(own, sib, both, sem):
    copies = [pltpu.make_async_copy(v, both.at[pl.ds(8 * i, 8)], sem.at[i]) for i, v in enumerate((own, sib))]
    for copy in copies:
        copy.start()
    for copy in copies:
        copy.wait()


def select_kernel(group, n, tab, *refs):
    blocks, outs, sem = refs[:n], refs[n:-1], refs[-1]
    base = GROUPS[group][1] - n
    copies = []
    for out, k in zip(outs, [k for g, k in PARTS if g == group]):
        low, high = rows_of(group, k)
        for j in range(low, high):
            for h in range(2):
                i = 2 * (j - low) + h
                b = tab[SEND + 16 * k + 2 * j + h]
                copies.append(pltpu.make_async_copy(blocks[j - base].at[b], out.at[i], sem.at[k, i]))
                copies[-1].start()
    for copy in copies:
        copy.wait()


def exact_rows(tab, both, kept, g_ref, total, peak, lse_ref):
    total[...] = jnp.zeros(total.shape, jnp.float32)
    peak[...] = jnp.full(peak.shape, floor_value, jnp.float32)

    def step(i, _):
        slot, s, t = pair_of(tab, i)
        x = tile_dot(kept[slot], both[s])
        if g_ref is not None:
            g = row_to_lanes(g_ref[pl.ds(t, 1), :])
            x = x + jnp.concatenate([g] * 4, axis=1)
        x = x * inv_epsilon
        high = jnp.max(x, axis=0, keepdims=True)
        mass = jnp.sum(jnp.exp(x - high), axis=0, keepdims=True)
        before = peak[pl.ds(s, 1), :]
        raised = jnp.maximum(before, high)
        total[pl.ds(s, 1), :] = total[pl.ds(s, 1), :] * jnp.exp(before - raised) + mass * jnp.exp(high - raised)
        peak[pl.ds(s, 1), :] = raised
        return 0

    lax.fori_loop(0, tab[COUNTS + len(TILES)], step, 0)
    for s in range(lse_ref.shape[0]):
        at = pl.ds(s, 1)
        lse_ref[at, :] = jnp.where(tab[HAS + s] > 0, peak[at, :] + jnp.log(total[at, :]), floor_value)


def finish_rows(tab, acc, before, lse_ref):
    ok = jnp.ones((1, lse_ref.shape[1]), jnp.float32)
    for s in range(acc.shape[0]):
        mass = jnp.sum(acc[s], axis=0, keepdims=True)
        if before is not None:
            mass = mass + before[pl.ds(s, 1), :]
        empty = tab[HAS + s] == 0
        fine = empty | ((mass >= sum_low) & (mass <= sum_high))
        ok = jnp.minimum(ok, jnp.where(fine, 1.0, 0.0))
        lse_ref[pl.ds(s, 1), :] = jnp.where(empty, floor_value, jnp.log(mass))
    return jnp.min(ok) > 0.5


def tile_kernel(group, tab, both, *refs):
    last = group == len(TILES) - 1
    base = 8 * TILES[group][0][0]
    here = parts_of(group)
    parts, refs = refs[: len(here)], refs[len(here) :]
    if group > 0:
        sums_in, refs = refs[0], refs[3:]
    k_out, kept, sums, acc, t_sem = refs[:5]

    def fetch(slot, block):
        return pltpu.make_async_copy(block, kept.at[slot], t_sem.at[slot - base])

    for part, (g, k) in zip(parts, here):
        low = rows_of(g, k)[0]
        for j in range(*rows_of(g, k)):
            for h in range(2):
                slot = 8 * j + 2 * k + h

                @pl.when(tab[CODE + slot] >= 0)
                def _():
                    fetch(slot, part.at[2 * (j - low) + h]).start()

    acc[...] = jnp.zeros(acc.shape, jnp.float32)

    start, stop = tab[COUNTS + group], tab[COUNTS + group + 1]

    def body(i, live):
        slot, s, _ = pair_of(tab, i)
        k = jnp.exp(tile_dot(kept[slot], both[s]) * inv_epsilon)
        k_out[slot] = k
        acc[s] = acc[s] + fold(k) * live.astype(jnp.float32)

    batched(start, stop, 4, lambda i: fetch(tab[LIST + i], parts[0].at[0]).wait(), body)
    if last:
        ok = finish_rows(tab, acc, sums_in, sums)
    else:
        for s in range(acc.shape[0]):
            mass = jnp.sum(acc[s], axis=0, keepdims=True)
            sums[pl.ds(s, 1), :] = mass if group == 0 else mass + sums_in[pl.ds(s, 1), :]

    if last:
        total, peak = refs[5:]

        @pl.when(jnp.logical_not(ok))
        def _():
            exact_rows(tab, both, kept, None, total, peak, sums)


def row_kernel(tab, g_in, k_in, both, kept, lse_ref, gbuf, vbuf, acc, total, peak):
    acc[...] = jnp.zeros(acc.shape, jnp.float32)
    gbuf[pl.ds(0, CHIPS), :] = g_in[:, :128]
    gbuf[pl.ds(CHIPS, CHIPS), :] = g_in[:, 128:]
    scaled = gbuf[...] * inv_epsilon
    vbuf[...] = jnp.exp(scaled)
    fits = all_true((scaled >= pot_low) & (scaled <= pot_high))

    def body(i, live):
        slot, s, t = pair_of(tab, i)
        v = row_to_lanes(vbuf[pl.ds(t, 1), :] * live.astype(jnp.float32))
        part = [fold(k * v) for k in quarters(k_in.at[slot])]
        acc[s] = acc[s] + jnp.concatenate(part, axis=1)

    batched(0, tab[COUNTS + len(TILES)], 8, None, body)
    ok = finish_rows(tab, acc, None, lse_ref)

    @pl.when(jnp.logical_not(ok & fits))
    def _():
        exact_rows(tab, both, kept, gbuf, total, peak, lse_ref)


def column_kernel(
    tab, l0, l1, l2, l3, log_a, log_a_sib, k_in, both, kept, f_ref, lse_ref, ubuf, mass, lse
):
    a, b, c, d = l0[...], l1[...], l2[...], l3[...]
    top = jnp.maximum(jnp.maximum(a, c), jnp.maximum(b, d))
    summed = (jnp.exp(a - top) + jnp.exp(c - top)) + (jnp.exp(b - top) + jnp.exp(d - top))
    weights = jnp.concatenate([log_a[...], log_a_sib[...]], axis=0)
    f = epsilon * weights - epsilon * (top + jnp.log(summed))
    f_ref[...] = f[:8]
    scaled = f * inv_epsilon
    fits = all_true((scaled >= pot_low) & (scaled <= pot_high))
    ubuf[...] = jnp.exp(scaled)
    mass[...] = jnp.full(mass.shape, -1.0, jnp.float32)

    def body(i, live):
        slot, s, t = pair_of(tab, i)
        us = quarters(ubuf[pl.ds(s, 1), :])
        ks = quarters(k_in.at[slot])
        part = (ks[0] * us[0] + ks[1] * us[1]) + (ks[2] * us[2] + ks[3] * us[3])
        mass[pl.ds(t, 1), :] = lanes_to_row(part)

    batched(0, tab[COUNTS + len(TILES)], 8, None, body)
    m = mass[...]
    dead = m == -1.0
    ok = all_true(dead | ((m >= sum_low) & (m <= sum_high)))
    lse[...] = jnp.where(dead, floor_value, jnp.log(m))

    @pl.when(jnp.logical_not(ok & fits))
    def _():
        ubuf[...] = f

        def exact(i, _):
            slot, s, t = pair_of(tab, i)
            x = (ubuf[pl.ds(s, 1), :] + tile_dot(kept[slot], both[s])) * inv_epsilon
            high = jnp.max(x, axis=1, keepdims=True)
            column = high + jnp.log(jnp.sum(jnp.exp(x - high), axis=1, keepdims=True))
            lse[pl.ds(t, 1), :] = jnp.broadcast_to(column, (128, 128)).T[:1, :]
            return 0

        lax.fori_loop(0, tab[COUNTS + len(TILES)], exact, 0)

    lse_ref[:, :128] = lse[pl.ds(0, CHIPS), :]
    lse_ref[:, 128:] = lse[pl.ds(CHIPS, CHIPS), :]


def owner_kernel(parts, wanted, log_b, g_ref, back):
    halves = [parts[:, :128], parts[:, 128:]]
    asked = [jnp.broadcast_to(wanted[:, h : h + 1], halves[h].shape) for h in range(2)]
    outs = [jnp.zeros(halves[h].shape, jnp.float32) for h in range(2)]
    for j in range(g_ref.shape[0]):
        hits = [w == j for w in asked]
        top = functools.reduce(
            jnp.maximum,
            [jnp.max(jnp.where(hit, x, floor_value), axis=0, keepdims=True) for hit, x in zip(hits, halves)],
        )
        mass = sum(
            jnp.sum(jnp.where(hit, jnp.exp(x - top), 0.0), axis=0, keepdims=True) for hit, x in zip(hits, halves)
        )
        g = epsilon * log_b[pl.ds(j, 1), :] - epsilon * (top + jnp.log(mass))
        g_ref[pl.ds(j, 1), :] = g
        outs = [jnp.where(hit, g, out) for hit, out in zip(hits, outs)]
    back[:, :128] = outs[0]
    back[:, 128:] = outs[1]


def shift(value, axis, by):
    n = lax.axis_size(axis)
    return lax.ppermute(value, axis, [(i, (i + by) % n) for i in range(n)])


def per_device(source, targets, log_a, log_b, pair_source, pair_target, pair_count):
    xi, zi, core = (lax.axis_index(a) for a in ("x", "z", "core"))
    local_blocks, quarter, width = targets.shape
    blocks, rows, _ = source.shape
    f32, i32, bf16 = jnp.float32, jnp.int32, jnp.bfloat16
    sds = jax.ShapeDtypeStruct

    def params(mib):
        return pltpu.CompilerParams(vmem_limit_bytes=mib * MIB)

    pin = pltpu.with_memory_space_constraint

    def swap_cores(v):
        return shift(v, "core", 1)

    owners = pair_target.shape[0]
    live = lax.broadcasted_iota(i32, pair_target.shape, 1) < pair_count[:, None]
    match = live[:, None, :] & ((pair_target // local_blocks)[:, None, :] == jnp.arange(owners, dtype=i32)[None, :, None])
    named = jnp.max(jnp.where(match, (pair_source * local_blocks + pair_target % local_blocks)[:, None, :], -1), axis=2)
    tab = pl.pallas_call(table_kernel, out_shape=sds((TABLE,), i32), in_specs=[SM], out_specs=SM)(named)
    tab = pin(tab, pltpu.HBM)
    wanted = lax.dynamic_index_in_dim(named, 2 * (xi * ZS + zi) + core, 1, keepdims=False).reshape(CHIPS, 2)
    wanted = jnp.where(core == 0, wanted, wanted[:, ::-1])
    wanted = jnp.where(wanted >= 0, wanted & 3, -1)

    sib = swap_cores(source)
    log_a_sib = swap_cores(log_a)
    p1, m1 = shift(targets, "z", 1), shift(targets, "z", -1)
    p1, m1, tab = lax.optimization_barrier((p1, m1, tab))
    p2, m2 = shift(p1, "z", 1), shift(m1, "z", -1)

    def select(group, *blocks):
        n = len(blocks)
        spans = [rows_of(group, k) for g, k in PARTS if g == group]
        return pl.pallas_call(
            functools.partial(select_kernel, group, n),
            out_shape=[pltpu.VMEM((2 * (high - low), quarter, width), bf16) for low, high in spans],
            in_specs=[SM] + [ANY] * n,
            out_specs=[ANY] * len(spans),
            scratch_shapes=[pltpu.SemaphoreType.DMA((XS, 2 * len(DZ)))],
            compiler_params=params(4),
        )(tab, *[pin(v, pltpu.VMEM) for v in blocks])

    def along_x(group, blocks):
        ks = [k for g, k in PARTS if g == group]
        return {(group, k): shift(v, "x", DX[k]) if k else v for k, v in zip(ks, blocks)}

    first = along_x(0, select(0, targets))
    p3, m3 = shift(p2, "z", 1), shift(m2, "z", -1)
    p4 = shift(p3, "z", 1)
    second = select(1, targets, p1, m1, p2, m2)
    second, first = lax.optimization_barrier((second, first))
    second = along_x(1, second)
    third = along_x(2, select(2, targets, p1, m1, p2, m2, p3, m3, p4))
    held = {**first, **{p: pin(v, pltpu.VMEM) for p, v in (*second.items(), *third.items())}}

    tiles = (SLOTS, quarter, rows)
    kept = (SLOTS, quarter, width)
    both = 2 * blocks
    row_scratch = [pltpu.VMEM((both, rows), f32)] * 2
    acc = pltpu.VMEM((both, 8, rows), f32)

    sources = pl.pallas_call(
        stack_kernel,
        out_shape=pltpu.VMEM((both, rows, width), bf16),
        in_specs=[ANY, ANY],
        out_specs=VM,
        scratch_shapes=[pltpu.SemaphoreType.DMA((2,))],
        compiler_params=params(1),
    )(pin(source, pltpu.HBM), sib)

    def tile_call(group, before):
        slots = 8 * (TILES[group][-1][0] + 1 - TILES[group][0][0])
        parts = [held[p] for p in parts_of(group)]
        ins = [tab, pin(sources, pltpu.VMEM), *parts]
        specs = [SM, VM] + [ANY] * (len(ins) - 2)
        alias = {}
        if before:
            k_tiles, kept_rows, sums = before
            ins += [sums, pin(k_tiles, pltpu.VMEM), pin(kept_rows, pltpu.VMEM)]
            specs += [VM, VM, VM]
            alias = {len(ins) - 2: 0, len(ins) - 1: 1}
        scratch = [acc, pltpu.SemaphoreType.DMA((slots,))]
        if group == len(TILES) - 1:
            scratch += row_scratch
        return pl.pallas_call(
            functools.partial(tile_kernel, group),
            out_shape=(pltpu.VMEM(tiles, f32), pltpu.VMEM(kept, bf16), sds((both, rows), f32)),
            in_specs=specs,
            out_specs=(VM, VM, VM),
            scratch_shapes=scratch,
            input_output_aliases=alias,
            compiler_params=params(4),
            cost_estimate=pl.CostEstimate(
                flops=slots * rows * quarter * width, bytes_accessed=10 * MIB, transcendentals=slots * rows * quarter // 2
            ),
        )(*ins)

    k_tiles, kept_rows, sums = tile_call(0, None)
    sums, wanted, log_a_sib = lax.optimization_barrier((sums, wanted, log_a_sib))
    k_tiles, kept_rows, part = tile_call(1, (k_tiles, kept_rows, sums))

    resident = [pin(v, pltpu.VMEM) for v in (k_tiles, sources, kept_rows)]
    pots = pltpu.VMEM((SLOTS, quarter), f32)
    wide = (CHIPS, 2 * quarter)

    def columns(part):
        other = swap_cores(part)
        other = jnp.concatenate([other[blocks:], other[:blocks]])
        top = jnp.maximum(part, other)
        part = top + jnp.log(jnp.exp(part - top) + jnp.exp(other - top))
        one, three, two = (shift(part, "rep", k) for k in (1, 3, 2))
        parts = [part, one, two, three]
        return pl.pallas_call(
            column_kernel,
            out_shape=(sds((blocks, rows), f32), sds(wide, f32)),
            in_specs=[SM] + [VM] * 9,
            out_specs=(VM, VM),
            scratch_shapes=[row_scratch[0], pots, pots],
            compiler_params=params(4),
        )(tab, *parts, log_a, log_a_sib, *resident)

    def swap(v):
        return lax.all_to_all(v, ("x", "z"), split_axis=0, concat_axis=0, tiled=True)

    def owner(parts):
        return pl.pallas_call(
            owner_kernel,
            out_shape=(sds((local_blocks, quarter), f32), sds(wide, f32)),
            in_specs=[VM, VM, VM],
            out_specs=(VM, VM),
            compiler_params=params(4),
        )(parts, wanted, log_b)

    f, col = columns(part)
    g, back = owner(swap(col))
    part = pl.pallas_call(
        row_kernel,
        out_shape=sds((both, rows), f32),
        in_specs=[SM] + [VM] * 4,
        out_specs=VM,
        scratch_shapes=[pots, pots, acc, *row_scratch],
        compiler_params=params(4),
    )(tab, swap(back), *resident)
    f, col = columns(part)
    g, _ = owner(swap(col))
    return f, g


def solution(mesh):
    fine = Mesh(mesh.devices.reshape(XS, ZS, 2, 4), ("x", "z", "core", "rep"))
    blk = ("x", "z", "core")
    in_specs = (P(blk, None, None), P(blk, "rep", None), P(blk, None), P(blk, "rep"), P(), P(), P())
    out_specs = (P(blk, None), P(blk, "rep"))
    return jax.shard_map(per_device, mesh=fine, in_specs=in_specs, out_specs=out_specs, check_vma=False)
```

```python
import functools

import jax
import jax.numpy as jnp
from jax import lax
from jax.experimental import pallas as pl
from jax.experimental.pallas import tpu as pltpu
from jax.sharding import Mesh, PartitionSpec as P

epsilon = 0.1
inv_epsilon = 10.0
floor_value = -1e30
sum_low, sum_high = 1e-13, 1e26
pot_low, pot_high = -80.0, 35.0

VM = pl.BlockSpec(memory_space=pltpu.VMEM)
SM = pl.BlockSpec(memory_space=pltpu.SMEM)
ANY = pl.BlockSpec(memory_space=pl.ANY)
MIB = 1024 * 1024

XS, ZS = 4, 8
CHIPS = XS * ZS
DZ = (0, 1, 7, 2, 6, 3, 5, 4)
DX = (0, 1, 3, 2)
GROUPS = ((0, 1), (1, 5), (5, 8))


def rows_of(group, k):
    if k == 0:
        return ((0, 0), (0, 0), (0, len(DZ)))[group]
    if k == XS - 1 and group < 2:
        return ((0, 0), (0, GROUPS[1][1]))[group]
    return GROUPS[group]


PARTS = [(g, k) for g in range(len(GROUPS)) for k in range(XS) if rows_of(g, k)[0] < rows_of(g, k)[1]]
TILES = (
    [(j, k) for j in range(len(DZ)) for k in range(XS) if j < GROUPS[2][0] or k == 0],
    [(j, k) for j in range(*GROUPS[2]) for k in range(1, XS)],
)


def parts_of(group):
    return [(g, k) for g, k in PARTS if any((j, k) in TILES[group] for j in range(*rows_of(g, k)))]


SLOTS = 2 * CHIPS
CODE, LIST, TROW, SEND, HAS, COUNTS, TABLE = 0, 64, 128, 160, 224, 241, 256


def tile_dot(left, right):
    return lax.dot_general(left, right, (((1,), (1,)), ((), ())), preferred_element_type=jnp.float32)


def all_true(mask):
    return jnp.min(jnp.where(mask, 1.0, 0.0)) > 0.5


def row_to_lanes(row):
    return jnp.broadcast_to(row, (128, 128)).T


def lanes_to_row(tile):
    return jnp.sum(tile.T, axis=0, keepdims=True)


def fold(tile):
    return jnp.sum(tile.reshape(16, 8, tile.shape[1]), axis=0)


def quarters(tile):
    return [tile[:, 128 * q : 128 * (q + 1)] for q in range(4)]


def batched(start, stop, width, wait, body):
    def step(q, _):
        base = start + q * width
        for w in range(width if wait else 0):

            @pl.when(base + w < stop)
            def _():
                wait(base + w)

        for w in range(width):
            body(jnp.minimum(base + w, stop - 1), base + w < stop)
        return 0

    lax.fori_loop(0, (stop - start + width - 1) // width, step, 0)


def pair_of(tab, i):
    slot = tab[LIST + i]
    h = slot & 1
    return slot, h * 8 + (tab[CODE + slot] >> 2), h * CHIPS + tab[TROW + (slot >> 1)]


def table_kernel(named, tab):
    x, z, c = (lax.axis_index(a) for a in ("x", "z", "core"))
    for i in range(HAS, TABLE):
        tab[i] = 0
    count = 0
    for group in range(len(TILES)):
        for j, k in TILES[group]:
            r = XS * j + k
            row = ((x - DX[k]) & (XS - 1)) * ZS + ((z - DZ[j]) & (ZS - 1))
            tab[TROW + r] = row
            for h in range(2):
                code = named[2 * (x * ZS + z) + (c ^ h), 2 * row + c]
                live = code >= 0
                tab[CODE + 2 * r + h] = code
                tab[LIST + count] = 2 * r + h
                count = count + live.astype(jnp.int32)
                tab[jnp.where(live, HAS + h * 8 + (code >> 2), HAS + 16)] = 1
        tab[COUNTS + 1 + group] = count
    for j, dz in enumerate(DZ):
        zt = (z - dz) & (ZS - 1)
        for k, dx in enumerate(DX):
            far = ((x + dx) & (XS - 1)) * ZS + z
            for h in range(2):
                code = named[2 * far + (c ^ h), 2 * (x * ZS + zt) + c]
                tab[SEND + 16 * k + 2 * j + h] = jnp.where(code >= 0, code & 3, 0)


def stack_kernel(own, sib, both, sem):
    copies = [pltpu.make_async_copy(v, both.at[pl.ds(8 * i, 8)], sem.at[i]) for i, v in enumerate((own, sib))]
    for copy in copies:
        copy.start()
    for copy in copies:
        copy.wait()


def select_kernel(group, n, tab, *refs):
    blocks, outs, sem = refs[:n], refs[n:-1], refs[-1]
    base = GROUPS[group][1] - n
    copies = []
    for out, k in zip(outs, [k for g, k in PARTS if g == group]):
        low, high = rows_of(group, k)
        for j in range(low, high):
            for h in range(2):
                i = 2 * (j - low) + h
                b = tab[SEND + 16 * k + 2 * j + h]
                copies.append(pltpu.make_async_copy(blocks[j - base].at[b], out.at[i], sem.at[k, i]))
                copies[-1].start()
    for copy in copies:
        copy.wait()


def exact_rows(tab, both, kept, g_ref, total, peak, lse_ref):
    total[...] = jnp.zeros(total.shape, jnp.float32)
    peak[...] = jnp.full(peak.shape, floor_value, jnp.float32)

    def step(i, _):
        slot, s, t = pair_of(tab, i)
        x = tile_dot(kept[slot], both[s])
        if g_ref is not None:
            g = row_to_lanes(g_ref[pl.ds(t, 1), :])
            x = x + jnp.concatenate([g] * 4, axis=1)
        x = x * inv_epsilon
        high = jnp.max(x, axis=0, keepdims=True)
        mass = jnp.sum(jnp.exp(x - high), axis=0, keepdims=True)
        before = peak[pl.ds(s, 1), :]
        raised = jnp.maximum(before, high)
        total[pl.ds(s, 1), :] = total[pl.ds(s, 1), :] * jnp.exp(before - raised) + mass * jnp.exp(high - raised)
        peak[pl.ds(s, 1), :] = raised
        return 0

    lax.fori_loop(0, tab[COUNTS + len(TILES)], step, 0)
    for s in range(lse_ref.shape[0]):
        at = pl.ds(s, 1)
        lse_ref[at, :] = jnp.where(tab[HAS + s] > 0, peak[at, :] + jnp.log(total[at, :]), floor_value)


def finish_rows(tab, acc, before, lse_ref):
    ok = jnp.ones((1, lse_ref.shape[1]), jnp.float32)
    for s in range(acc.shape[0]):
        mass = jnp.sum(acc[s], axis=0, keepdims=True)
        if before is not None:
            mass = mass + before[pl.ds(s, 1), :]
        empty = tab[HAS + s] == 0
        fine = empty | ((mass >= sum_low) & (mass <= sum_high))
        ok = jnp.minimum(ok, jnp.where(fine, 1.0, 0.0))
        lse_ref[pl.ds(s, 1), :] = jnp.where(empty, floor_value, jnp.log(mass))
    return jnp.min(ok) > 0.5


def tile_kernel(group, tab, both, *refs):
    last = group == len(TILES) - 1
    base = 8 * TILES[group][0][0]
    here = parts_of(group)
    parts, refs = refs[: len(here)], refs[len(here) :]
    if group > 0:
        sums_in, refs = refs[0], refs[3:]
    k_out, kept, sums, acc, t_sem = refs[:5]

    def fetch(slot, block):
        return pltpu.make_async_copy(block, kept.at[slot], t_sem.at[slot - base])

    for part, (g, k) in zip(parts, here):
        low = rows_of(g, k)[0]
        for j in range(*rows_of(g, k)):
            for h in range(2):
                slot = 8 * j + 2 * k + h

                @pl.when(tab[CODE + slot] >= 0)
                def _():
                    fetch(slot, part.at[2 * (j - low) + h]).start()

    acc[...] = jnp.zeros(acc.shape, jnp.float32)

    start, stop = tab[COUNTS + group], tab[COUNTS + group + 1]

    def body(i, live):
        slot, s, _ = pair_of(tab, i)
        k = jnp.exp(tile_dot(kept[slot], both[s]) * inv_epsilon)
        k_out[slot] = k
        acc[s] = acc[s] + fold(k) * live.astype(jnp.float32)

    batched(start, stop, 4, lambda i: fetch(tab[LIST + i], parts[0].at[0]).wait(), body)
    if last:
        ok = finish_rows(tab, acc, sums_in, sums)
    else:
        for s in range(acc.shape[0]):
            mass = jnp.sum(acc[s], axis=0, keepdims=True)
            sums[pl.ds(s, 1), :] = mass if group == 0 else mass + sums_in[pl.ds(s, 1), :]

    if last:
        total, peak = refs[5:]

        @pl.when(jnp.logical_not(ok))
        def _():
            exact_rows(tab, both, kept, None, total, peak, sums)


def row_kernel(tab, g_in, k_in, both, kept, lse_ref, gbuf, vbuf, acc, total, peak):
    acc[...] = jnp.zeros(acc.shape, jnp.float32)
    gbuf[pl.ds(0, CHIPS), :] = g_in[:, :128]
    gbuf[pl.ds(CHIPS, CHIPS), :] = g_in[:, 128:]
    scaled = gbuf[...] * inv_epsilon
    vbuf[...] = jnp.exp(scaled)
    fits = all_true((scaled >= pot_low) & (scaled <= pot_high))

    def body(i, live):
        slot, s, t = pair_of(tab, i)
        v = row_to_lanes(vbuf[pl.ds(t, 1), :] * live.astype(jnp.float32))
        part = [fold(k * v) for k in quarters(k_in.at[slot])]
        acc[s] = acc[s] + jnp.concatenate(part, axis=1)

    batched(0, tab[COUNTS + len(TILES)], 8, None, body)
    ok = finish_rows(tab, acc, None, lse_ref)

    @pl.when(jnp.logical_not(ok & fits))
    def _():
        exact_rows(tab, both, kept, gbuf, total, peak, lse_ref)


def column_kernel(
    tab, l0, l1, l2, l3, log_a, log_a_sib, k_in, both, kept, f_ref, lse_ref, ubuf, mass, lse
):
    a, b, c, d = l0[...], l1[...], l2[...], l3[...]
    top = jnp.maximum(jnp.maximum(a, c), jnp.maximum(b, d))
    summed = (jnp.exp(a - top) + jnp.exp(c - top)) + (jnp.exp(b - top) + jnp.exp(d - top))
    weights = jnp.concatenate([log_a[...], log_a_sib[...]], axis=0)
    f = epsilon * weights - epsilon * (top + jnp.log(summed))
    f_ref[...] = f[:8]
    scaled = f * inv_epsilon
    fits = all_true((scaled >= pot_low) & (scaled <= pot_high))
    ubuf[...] = jnp.exp(scaled)
    mass[...] = jnp.full(mass.shape, -1.0, jnp.float32)

    def body(i, live):
        slot, s, t = pair_of(tab, i)
        us = quarters(ubuf[pl.ds(s, 1), :])
        ks = quarters(k_in.at[slot])
        part = (ks[0] * us[0] + ks[1] * us[1]) + (ks[2] * us[2] + ks[3] * us[3])
        mass[pl.ds(t, 1), :] = lanes_to_row(part)

    batched(0, tab[COUNTS + len(TILES)], 8, None, body)
    m = mass[...]
    dead = m == -1.0
    ok = all_true(dead | ((m >= sum_low) & (m <= sum_high)))
    lse[...] = jnp.where(dead, floor_value, jnp.log(m))

    @pl.when(jnp.logical_not(ok & fits))
    def _():
        ubuf[...] = f

        def exact(i, _):
            slot, s, t = pair_of(tab, i)
            x = (ubuf[pl.ds(s, 1), :] + tile_dot(kept[slot], both[s])) * inv_epsilon
            high = jnp.max(x, axis=1, keepdims=True)
            column = high + jnp.log(jnp.sum(jnp.exp(x - high), axis=1, keepdims=True))
            lse[pl.ds(t, 1), :] = jnp.broadcast_to(column, (128, 128)).T[:1, :]
            return 0

        lax.fori_loop(0, tab[COUNTS + len(TILES)], exact, 0)

    lse_ref[:, :128] = lse[pl.ds(0, CHIPS), :]
    lse_ref[:, 128:] = lse[pl.ds(CHIPS, CHIPS), :]


def owner_kernel(parts, wanted, log_b, g_ref, back=None):
    halves = [parts[:, :128], parts[:, 128:]]
    asked = [jnp.broadcast_to(wanted[:, h : h + 1], halves[h].shape) for h in range(2)]
    outs = [jnp.zeros(halves[h].shape, jnp.float32) for h in range(2)]
    for j in range(g_ref.shape[0]):
        hits = [w == j for w in asked]
        top = functools.reduce(
            jnp.maximum,
            [jnp.max(jnp.where(hit, x, floor_value), axis=0, keepdims=True) for hit, x in zip(hits, halves)],
        )
        mass = sum(
            jnp.sum(jnp.where(hit, jnp.exp(x - top), 0.0), axis=0, keepdims=True) for hit, x in zip(hits, halves)
        )
        g = epsilon * log_b[pl.ds(j, 1), :] - epsilon * (top + jnp.log(mass))
        g_ref[pl.ds(j, 1), :] = g
        outs = [jnp.where(hit, g, out) for hit, out in zip(hits, outs)]
    if back is not None:
        back[:, :128] = outs[0]
        back[:, 128:] = outs[1]


def shift(value, axis, by):
    n = lax.axis_size(axis)
    return lax.ppermute(value, axis, [(i, (i + by) % n) for i in range(n)])


def per_device(source, targets, log_a, log_b, pair_source, pair_target, pair_count):
    xi, zi, core = (lax.axis_index(a) for a in ("x", "z", "core"))
    local_blocks, quarter, width = targets.shape
    blocks, rows, _ = source.shape
    f32, i32, bf16 = jnp.float32, jnp.int32, jnp.bfloat16
    sds = jax.ShapeDtypeStruct

    def params(mib):
        return pltpu.CompilerParams(vmem_limit_bytes=mib * MIB)

    pin = pltpu.with_memory_space_constraint

    def swap_cores(v):
        return shift(v, "core", 1)

    owners = pair_target.shape[0]
    live = lax.broadcasted_iota(i32, pair_target.shape, 1) < pair_count[:, None]
    match = live[:, None, :] & ((pair_target // local_blocks)[:, None, :] == jnp.arange(owners, dtype=i32)[None, :, None])
    named = jnp.max(jnp.where(match, (pair_source * local_blocks + pair_target % local_blocks)[:, None, :], -1), axis=2)
    tab = pl.pallas_call(table_kernel, out_shape=sds((TABLE,), i32), in_specs=[SM], out_specs=SM)(named)
    tab = pin(tab, pltpu.HBM)
    wanted = lax.dynamic_index_in_dim(named, 2 * (xi * ZS + zi) + core, 1, keepdims=False).reshape(CHIPS, 2)
    wanted = jnp.where(core == 0, wanted, wanted[:, ::-1])
    wanted = jnp.where(wanted >= 0, wanted & 3, -1)

    sib = swap_cores(source)
    log_a_sib = swap_cores(log_a)
    p1, m1 = shift(targets, "z", 1), shift(targets, "z", -1)
    p1, m1, tab = lax.optimization_barrier((p1, m1, tab))
    p2, m2 = shift(p1, "z", 1), shift(m1, "z", -1)

    def select(group, *blocks):
        n = len(blocks)
        spans = [rows_of(group, k) for g, k in PARTS if g == group]
        return pl.pallas_call(
            functools.partial(select_kernel, group, n),
            out_shape=[pltpu.VMEM((2 * (high - low), quarter, width), bf16) for low, high in spans],
            in_specs=[SM] + [ANY] * n,
            out_specs=[ANY] * len(spans),
            scratch_shapes=[pltpu.SemaphoreType.DMA((XS, 2 * len(DZ)))],
            compiler_params=params(4),
        )(tab, *[pin(v, pltpu.VMEM) for v in blocks])

    def along_x(group, blocks):
        ks = [k for g, k in PARTS if g == group]
        return {(group, k): shift(v, "x", DX[k]) if k else v for k, v in zip(ks, blocks)}

    first = along_x(0, select(0, targets))
    p3, m3 = shift(p2, "z", 1), shift(m2, "z", -1)
    p4 = shift(p3, "z", 1)
    second = select(1, targets, p1, m1, p2, m2)
    second, first = lax.optimization_barrier((second, first))
    second = along_x(1, second)
    third = along_x(2, select(2, targets, p1, m1, p2, m2, p3, m3, p4))
    held = {**first, **{p: pin(v, pltpu.VMEM) for p, v in (*second.items(), *third.items())}}

    tiles = (SLOTS, quarter, rows)
    kept = (SLOTS, quarter, width)
    both = 2 * blocks
    row_scratch = [pltpu.VMEM((both, rows), f32)] * 2
    acc = pltpu.VMEM((both, 8, rows), f32)

    sources = pl.pallas_call(
        stack_kernel,
        out_shape=pltpu.VMEM((both, rows, width), bf16),
        in_specs=[ANY, ANY],
        out_specs=VM,
        scratch_shapes=[pltpu.SemaphoreType.DMA((2,))],
        compiler_params=params(1),
    )(pin(source, pltpu.HBM), sib)

    def tile_call(group, before):
        slots = 8 * (TILES[group][-1][0] + 1 - TILES[group][0][0])
        parts = [held[p] for p in parts_of(group)]
        ins = [tab, pin(sources, pltpu.VMEM), *parts]
        specs = [SM, VM] + [ANY] * (len(ins) - 2)
        alias = {}
        if before:
            k_tiles, kept_rows, sums = before
            ins += [sums, pin(k_tiles, pltpu.VMEM), pin(kept_rows, pltpu.VMEM)]
            specs += [VM, VM, VM]
            alias = {len(ins) - 2: 0, len(ins) - 1: 1}
        scratch = [acc, pltpu.SemaphoreType.DMA((slots,))]
        if group == len(TILES) - 1:
            scratch += row_scratch
        return pl.pallas_call(
            functools.partial(tile_kernel, group),
            out_shape=(pltpu.VMEM(tiles, f32), pltpu.VMEM(kept, bf16), sds((both, rows), f32)),
            in_specs=specs,
            out_specs=(VM, VM, VM),
            scratch_shapes=scratch,
            input_output_aliases=alias,
            compiler_params=params(4),
            cost_estimate=pl.CostEstimate(
                flops=slots * rows * quarter * width, bytes_accessed=10 * MIB, transcendentals=slots * rows * quarter // 2
            ),
        )(*ins)

    k_tiles, kept_rows, sums = tile_call(0, None)
    sums, wanted, log_a_sib = lax.optimization_barrier((sums, wanted, log_a_sib))
    k_tiles, kept_rows, part = tile_call(1, (k_tiles, kept_rows, sums))

    resident = [pin(v, pltpu.VMEM) for v in (k_tiles, sources, kept_rows)]
    pots = pltpu.VMEM((SLOTS, quarter), f32)
    wide = (CHIPS, 2 * quarter)

    def columns(part):
        other = swap_cores(part)
        other = jnp.concatenate([other[blocks:], other[:blocks]])
        top = jnp.maximum(part, other)
        part = top + jnp.log(jnp.exp(part - top) + jnp.exp(other - top))
        one, three, two = (shift(part, "rep", k) for k in (1, 3, 2))
        parts = [part, one, two, three]
        return pl.pallas_call(
            column_kernel,
            out_shape=(sds((blocks, rows), f32), sds(wide, f32)),
            in_specs=[SM] + [VM] * 9,
            out_specs=(VM, VM),
            scratch_shapes=[row_scratch[0], pots, pots],
            compiler_params=params(4),
        )(tab, *parts, log_a, log_a_sib, *resident)

    def swap(v):
        return lax.all_to_all(v, ("x", "z"), split_axis=0, concat_axis=0, tiled=True)

    def owner(parts, last):
        shapes = (sds((local_blocks, quarter), f32), sds(wide, f32))
        return pl.pallas_call(
            owner_kernel,
            out_shape=shapes[:1] if last else shapes,
            in_specs=[VM, VM, VM],
            out_specs=(VM,) if last else (VM, VM),
            compiler_params=params(4),
        )(parts, wanted, log_b)

    f, col = columns(part)
    g, back = owner(swap(col), False)
    part = pl.pallas_call(
        row_kernel,
        out_shape=sds((both, rows), f32),
        in_specs=[SM] + [VM] * 4,
        out_specs=VM,
        scratch_shapes=[pots, pots, acc, *row_scratch],
        compiler_params=params(4),
    )(tab, swap(back), *resident)
    f, col = columns(part)
    (g,) = owner(swap(col), True)
    return f, g


def solution(mesh):
    fine = Mesh(mesh.devices.reshape(XS, ZS, 2, 4), ("x", "z", "core", "rep"))
    blk = ("x", "z", "core")
    in_specs = (P(blk, None, None), P(blk, "rep", None), P(blk, None), P(blk, "rep"), P(), P(), P())
    out_specs = (P(blk, None), P(blk, "rep"))
    return jax.shard_map(per_device, mesh=fine, in_specs=in_specs, out_specs=out_specs, check_vma=False)
```
